256 devices in a mesh: seq: 32 (over x, y, core), ch: 8 (over z).
Axes of the slice: x: 4, y: 4, z: 8, core: 2. Of those that a mesh axis runs over, the one named last changes fastest.
Arguments:
- query_proj: bfloat16 [8192, 8192], P('seq', 'ch'), may hold values from -6 to 6
- key_projected: bfloat16 [8192, 8192], P('seq', 'ch'), may hold values from -6 to 6
- value_projected: bfloat16 [8192, 8192], P('seq', 'ch'), may hold values from -6 to 6
- mode_decay_speed: float32 [8192, 16], P('ch'), may hold values from 6.1035156e-05 to 0.04
- residue: float32 [8192, 16], P('ch'), may hold values from -1.5 to 1.5
- out_weight: bfloat16 [8192, 4096], P('ch'), may hold values from -0.09375 to 0.09375
Outputs:
- projected: bfloat16 [8192, 4096], P('seq', 'ch')
The draws below stay inside these ranges and needn't reach their ends.
All inputs are finite; a program needn't handle non-finite values.
Results may differ from the reference program's by a relative error of at most 0.023.
Values may be sent and summed in bfloat16 or wider, within the bound.
A program may use at most 192 MiB of HBM per device.

```python
import math
import jax
import jax.numpy as jnp
from jax import lax

CHANNELS = 8192
DOUT = 4096
MODES = 16
LENGTH = 8192


def raised(drawn, key, source, target, shards_of, factor):
    owner, partner = [(jnp.arange(drawn.shape[dim]) // (drawn.shape[dim] // shards_of)).reshape([-1 if axis == dim else 1 for axis in range(drawn.ndim)]) for dim in (source, target)]
    chosen = jax.random.permutation(key, shards_of)[partner]
    strong = (owner == chosen) | (owner == (partner + shards_of // 2) % shards_of)
    return jnp.where(strong, factor * drawn, drawn)


def steps_of(own_key, shape, shards, least, largest):
    level, own = 1.0, jax.random.fold_in(own_key, 6)
    for axis_at, parts in shards:
        draws = jnp.exp(jax.random.uniform(jax.random.fold_in(own, axis_at), (parts,), jnp.float32, least / len(shards), largest / len(shards)))
        level = level * jnp.repeat(draws, shape[axis_at] // parts).reshape([-1 if axis == axis_at else 1 for axis in range(len(shape))])
    return level


def normal_values(rng, extent, deviation, reach, split=(), held_as=jnp.bfloat16):
    values = jax.random.normal(rng, extent, jnp.float32) * deviation
    if len(split) > 0:
        values = steps_of(rng, extent, split, -0.22, 0.18) * values
    return jnp.clip(values, min=-reach, max=reach).astype(held_as)


def bell_draw_with(own_key, shape, spread, limit, cuts, heavy, kind=jnp.bfloat16):
    drawn = spread * jax.random.normal(own_key, shape, jnp.float32)
    if cuts:
        drawn = drawn * steps_of(own_key, shape, cuts, -0.22, 0.18)
    return jnp.clip(raised(drawn, jax.random.fold_in(own_key, 3), *heavy), -limit, limit).astype(kind)


def setup_inputs(seed: int = 0) -> dict:
    splits = jax.random.split(jax.random.key(seed), 7)
    return {
        "query_proj": normal_values(splits[0], (LENGTH, CHANNELS), 1.0, 6.0, ((0, 32), (1, 8))),
        "key_projected": normal_values(splits[1], (LENGTH, CHANNELS), 1.0, 6.0, ((0, 32), (1, 8))),
        "value_projected": normal_values(splits[2], (LENGTH, CHANNELS), 1.0, 6.0, ((0, 32), (1, 8))),
        "mode_decay_speed": jnp.clip(jnp.exp(math.log(0.04) - 6.4851847 * jax.random.uniform(splits[3], (CHANNELS, MODES), jnp.float32) ** steps_of(splits[3], (CHANNELS, MODES), ((0, 8),), -0.2, 0.2)), 6.103515625e-05, 0.04),
        "residue": normal_values(splits[4], (CHANNELS, MODES), 0.25, 1.5, ((0, 8),), jnp.float32),
        "out_weight": bell_draw_with(splits[5], (CHANNELS, DOUT), CHANNELS ** -0.5, 0.09375, ((0, 8),), (0, 1, 8, 2.0)),
    }


def filter_spectrum(frequency, mode_decay_speed, residue, length):
    half_angle = frequency.astype(jnp.float32) * (math.pi / (2 * length))
    sine_half = jnp.sin(half_angle)[..., None]
    sine_full = jnp.sin(2.0 * half_angle)[..., None]
    parity = (1 - 2 * (frequency % 2)).astype(jnp.float32)[..., None]
    total_real = jnp.zeros(frequency.shape + (mode_decay_speed.shape[0],), jnp.float32)
    total_imag = jnp.zeros(frequency.shape + (mode_decay_speed.shape[0],), jnp.float32)
    for mode_index in range(mode_decay_speed.shape[1]):
        rate = mode_decay_speed[:, mode_index]
        ratio = jnp.exp(-rate)
        one_minus = -jnp.expm1(-rate)
        weight_mode = residue[:, mode_index] * jnp.sqrt(-jnp.expm1(-2.0 * rate))
        tail = jnp.exp(-rate * length)
        den_real = one_minus + 2.0 * ratio * sine_half * sine_half
        den_imag = ratio * sine_full
        factor = weight_mode * (1.0 - tail * parity) / (den_real * den_real + den_imag * den_imag)
        total_real = total_real + factor * den_real
        total_imag = total_imag - factor * den_imag
    return (total_real, total_imag)

def reference(query_proj, key_projected, value_projected, mode_decay_speed, residue, out_weight):
    length = query_proj.shape[0]
    carried_signal = (key_projected.astype(jnp.float32) * value_projected.astype(jnp.float32)).astype(jnp.bfloat16)
    block_span_size = 64
    block_count = CHANNELS // block_span_size

    def one_block(block_index):
        leading_factor = block_index * block_span_size
        input_signal = lax.dynamic_slice_in_dim(carried_signal, leading_factor, block_span_size, 1).astype(jnp.float32)
        rates = lax.dynamic_slice_in_dim(mode_decay_speed, leading_factor, block_span_size, 0)
        weights = lax.dynamic_slice_in_dim(residue, leading_factor, block_span_size, 0)
        spectrum = jnp.fft.rfft(input_signal, n=2 * length, axis=0)
        frequency = jnp.arange(length + 1, dtype=jnp.int32)
        spec_real, spec_imag = filter_spectrum(frequency, rates, weights, length)
        product = spectrum * lax.complex(spec_real, spec_imag)
        return jnp.fft.irfft(product, n=2 * length, axis=0)[:length].astype(jnp.float32)
    blocks = lax.map(one_block, jnp.arange(block_count, dtype=jnp.int32))
    convolve_signal = jnp.moveaxis(blocks, 0, 1).reshape(length, CHANNELS)
    gated = (query_proj.astype(jnp.float32) * convolve_signal).astype(jnp.bfloat16)
    return jnp.dot(gated, out_weight, preferred_element_type=jnp.float32).astype(jnp.bfloat16)
```

```python
import functools

import jax
import jax.numpy as jnp
from jax import lax
from jax.experimental import pallas as pl
from jax.experimental.pallas import tpu as pltpu
from jax.sharding import PartitionSpec as P

MESH = pl.DeviceIdType.MESH
F32, BF16 = jnp.float32, jnp.bfloat16

ROWS = 256
WIDTH = 1024
COLS = 512
BLOCK = 64
CHIPS = 16

UNITS = [(0, 0), (1, 0), (2, 0), (3, 0), (0, 1), (1, 1), (2, 1), (3, 1), (0, 2), (1, 2), (2, 2), (3, 2), (0, 3), (1, 3)]
INDEX = {unit: at for at, unit in enumerate(UNITS)}


def distance(block, step):
    return (4 if block < 2 else 3) - step


def one_minus_exp(u):
    series = jnp.ones_like(u)
    for order in range(8, 1, -1):
        series = 1.0 - u * series * (1.0 / order)
    return jnp.where(u < 0.25, u * series, 1.0 - jnp.exp(-u))


def kernel(
    q_hbm, k_hbm, v_hbm, decay_hbm, residue_hbm, w_hbm, out_hbm,
    q_buf, k_buf, v_buf, decay_buf, residue_buf, w_buf,
    rate, ratio, weight, xs, ys, own, other, total, totals, carry, gated, part, sent, received, out_buf,
    load_sem, w_sem, core_send, core_recv, total_send, total_recv, carry_send, carry_recv, z_send, z_recv, out_sem,
):
    seq, z = lax.axis_index("seq"), lax.axis_index("ch")
    chip, core = lax.div(seq, 2), lax.rem(seq, 2)

    def device(chip_at, core_at):
        return {"seq": chip_at * 2 + core_at, "ch": z}

    def z_neighbour(direction):
        return {"seq": seq, "ch": lax.rem(z + (1 if direction == 0 else 7), 8)}

    barrier = pltpu.get_barrier_semaphore()
    for d in range(1, CHIPS):
        pl.semaphore_signal(barrier, inc=1, device_id=device(lax.rem(chip + d, CHIPS), core), device_id_type=MESH)
    pl.semaphore_signal(barrier, inc=1, device_id=device(chip, 1 - core), device_id_type=MESH)
    for direction in range(2):
        pl.semaphore_signal(barrier, inc=1, device_id=z_neighbour(direction), device_id_type=MESH)

    loads = [
        pltpu.make_async_copy(source, target, load_sem.at[at])
        for at, (source, target) in enumerate(
            [(decay_hbm, decay_buf), (k_hbm, k_buf), (v_hbm, v_buf), (residue_hbm, residue_buf), (q_hbm, q_buf)]
        )
    ]
    for load in loads:
        load.start()
    w_loads = {}
    for rd in (4, 5, 3, 2, 6, 1, 7, 0):
        columns = pl.ds(pl.multiple_of(lax.rem(z + rd, 8) * COLS, COLS), COLS)
        w_loads[rd] = pltpu.make_async_copy(w_hbm.at[:, columns], w_buf.at[rd], w_sem.at[rd])
        w_loads[rd].start()

    loads[0].wait()
    for j in range(8):
        rate[pl.ds(j, 16, stride=8), :] = decay_buf[pl.ds(128 * j, 128), :].T
    ratio[...] = jnp.exp(-rate[...])

    loads[1].wait()
    loads[2].wait()

    def carrier_rows(i, _):
        rows = pl.ds(pl.multiple_of(i * 16, 16), 16)
        product = (k_buf[rows, :].astype(F32) * v_buf[rows, :].astype(F32)).astype(BF16).astype(F32)
        for j in range(8):
            xs[pl.ds(i * 128 + j, 16, stride=8), :] = product[:, 128 * j : 128 * j + 128]
        return 0

    lax.fori_loop(0, ROWS // 16, carrier_rows, 0)

    def row(ref, t):
        return ref[pl.ds(pl.multiple_of(t * 8, 8), 8), :]

    def own_state(half):
        a = [row(ratio, half * 8 + n) for n in range(8)]
        a4 = [(s * s) * (s * s) for s in a]

        def four(i, state):
            x = [row(xs, 4 * i + r) for r in range(4)]
            return tuple(a4[n] * state[n] + (((a[n] * x[0] + x[1]) * a[n] + x[2]) * a[n] + x[3]) for n in range(8))

        state = lax.fori_loop(0, ROWS // 4, four, tuple(jnp.zeros((8, 128), F32) for _ in range(8)))
        for n in range(8):
            own[pl.ds(pl.multiple_of((half * 8 + n) * 8, 8), 8), :] = state[n]

    def half_rows(half):
        return pl.ds(pl.multiple_of(half * 64, 64), 64)

    def core_copy(half, at):
        return pltpu.make_async_remote_copy(
            src_ref=own.at[half_rows(half), :], dst_ref=other.at[half_rows(half), :],
            send_sem=core_send.at[at], recv_sem=core_recv.at[at], device_id=device(chip, 1 - core), device_id_type=MESH,
        )

    own_state(1 - core)
    pl.semaphore_wait(barrier, CHIPS - 1 + 1 + 2)
    first = core_copy(1 - core, 0)
    first.start()
    own_state(core)
    second = core_copy(core, 1)
    second.start()

    first.wait_recv()
    mine = half_rows(core)
    chunk = jnp.exp(rate[mine, :] * -float(ROWS))
    is_second = core == 1
    older = jnp.where(is_second, other[mine, :], own[mine, :])
    newer = jnp.where(is_second, own[mine, :], other[mine, :])
    total[...] = chunk * older + newer

    def total_copy(d):
        return pltpu.make_async_remote_copy(
            src_ref=total, dst_ref=totals.at[chip], send_sem=total_send.at[d], recv_sem=total_recv.at[chip],
            device_id=device(lax.rem(chip + d, CHIPS), core), device_id_type=MESH,
        )

    for d in range(CHIPS - 1, 0, -1):
        @pl.when(chip + d < CHIPS)
        def _():
            total_copy(d).start()

    loads[3].wait()
    for j in range(8):
        weight[pl.ds(j, 16, stride=8), :] = residue_buf[pl.ds(128 * j, 128), :].T
    weight[...] = weight[...] * jnp.sqrt(one_minus_exp(2.0 * rate[...]))

    for half in range(2):
        a = [row(ratio, half * 8 + n) for n in range(8)]
        w = [row(weight, half * 8 + n) for n in range(8)]

        def local_rows(i, state):
            for r in range(4):
                t = 4 * i + r
                x = row(xs, t)
                state = tuple(a[n] * state[n] + x for n in range(8))
                terms = [w[n] * state[n] for n in range(8)]
                y = ((terms[0] + terms[1]) + (terms[2] + terms[3])) + ((terms[4] + terms[5]) + (terms[6] + terms[7]))
                if half == 1:
                    y = y + row(ys, t)
                ys[pl.ds(pl.multiple_of(t * 8, 8), 8), :] = y
            return state

        lax.fori_loop(0, ROWS // 4, local_rows, tuple(jnp.zeros((8, 128), F32) for _ in range(8)))

    chip_decay = jnp.exp(rate[mine, :] * -float(2 * ROWS))

    def add_chip(p, state):
        pltpu.make_async_remote_copy(
            src_ref=total, dst_ref=totals.at[p], send_sem=total_send.at[0], recv_sem=total_recv.at[p],
            device_id=device(chip, 1 - core), device_id_type=MESH,
        ).wait_recv()
        return chip_decay * state + totals[p]

    carry[mine, :] = lax.fori_loop(0, chip, add_chip, jnp.zeros((64, 128), F32))
    carry_copy = pltpu.make_async_remote_copy(
        src_ref=carry.at[mine, :], dst_ref=carry.at[mine, :], send_sem=carry_send.at[0], recv_sem=carry_recv.at[0],
        device_id=device(chip, 1 - core), device_id_type=MESH,
    )
    carry_copy.start()
    second.wait_recv()
    loads[4].wait()
    carry_copy.wait_recv()

    before = jnp.where(is_second, jnp.exp(rate[...] * -float(ROWS)) * carry[...] + other[...], carry[...])
    own_carry = weight[...] * before

    def gate(block):
        start = own_carry * jnp.exp(rate[...] * -float(block * BLOCK))
        a = [row(ratio, n) for n in range(16)]

        def four(i, state):
            for r in range(4):
                t = block * BLOCK + 4 * i + r
                state = tuple(a[n] * state[n] for n in range(16))
                sums = [(state[4 * m] + state[4 * m + 1]) + (state[4 * m + 2] + state[4 * m + 3]) for m in range(4)]
                ys[pl.ds(pl.multiple_of(t * 8, 8), 8), :] = row(ys, t) + ((sums[0] + sums[1]) + (sums[2] + sums[3]))
            return state

        lax.fori_loop(0, BLOCK // 4, four, tuple(start[8 * n : 8 * n + 8] for n in range(16)))

        def sixteen(i, _):
            rows = pl.ds(pl.multiple_of(block * BLOCK + i * 16, 16), 16)
            for j in range(8):
                lanes = pl.ds(128 * j, 128)
                y = ys[pl.ds((block * BLOCK + i * 16) * 8 + j, 16, stride=8), :]
                gated[rows, lanes] = (q_buf[rows, lanes].astype(F32) * y).astype(BF16)
            return 0

        lax.fori_loop(0, BLOCK // 16, sixteen, 0)

    def rows_of(block):
        return pl.ds(block * BLOCK, BLOCK)

    def z_copy(direction, at):
        return pltpu.make_async_remote_copy(
            src_ref=sent.at[direction, at], dst_ref=received.at[direction, at],
            send_sem=z_send.at[direction, at], recv_sem=z_recv.at[direction, at],
            device_id=z_neighbour(direction), device_id_type=MESH,
        )

    def block_of(direction, block):
        return block if direction == 0 else (block + 2) % 4

    def relative(direction, block, step):
        return distance(block, step) if direction == 0 else 8 - distance(block, step)

    w_loads[4].wait()
    w_loads[5].wait()
    w_loads[3].wait()
    for block in (0, 2, 1, 3):
        gate(block)
        for direction in range(2):
            listed = block_of(direction, block)
            product = jnp.dot(gated[rows_of(block), :], w_buf[relative(direction, listed, 0)], preferred_element_type=F32)
            sent[direction, INDEX[listed, 0]] = product.astype(BF16)
            z_copy(direction, INDEX[listed, 0]).start()

    for rd in (2, 6, 1, 7, 0):
        w_loads[rd].wait()

    def products(k, _):
        rd = jnp.where(lax.rem(k, 2) == 0, 3 - lax.div(k, 2), 5 + lax.div(k, 2))
        for n in range(2):
            lanes = pl.ds(256 * n, 256)
            part[rd, :, lanes] = jnp.dot(gated[...], w_buf[rd, :, lanes], preferred_element_type=F32)
        return 0

    lax.fori_loop(0, 7, products, 0)

    for at, (listed, step) in enumerate(UNITS):
        if step == 0:
            continue
        for direction in range(2):
            block = block_of(direction, listed)
            previous = INDEX[listed, step - 1]
            z_copy(direction, previous).wait_recv()
            summed = part[relative(direction, listed, step), rows_of(block), :] + received[direction, previous].astype(F32)
            sent[direction, at] = summed.astype(BF16)
            z_copy(direction, at).start()

    outs = []
    for block in (0, 2, 1, 3):
        summed = part[0, rows_of(block), :]
        for direction in range(2):
            listed = block_of(direction, block)
            last = INDEX[listed, 3 if listed < 2 else 2]
            z_copy(direction, last).wait_recv()
            summed = summed + received[direction, last].astype(F32)
        out_buf[rows_of(block), :] = summed.astype(BF16)
        outs.append(pltpu.make_async_copy(out_buf.at[rows_of(block), :], out_hbm.at[rows_of(block), :], out_sem.at[block]))
        outs[-1].start()

    first.wait_send()
    second.wait_send()
    for d in range(1, CHIPS):
        @pl.when(chip + d < CHIPS)
        def _():
            total_copy(d).wait_send()
    carry_copy.wait_send()
    for direction in range(2):
        for at in range(len(UNITS)):
            z_copy(direction, at).wait_send()
    for out in outs:
        out.wait()


def per_device(query_proj, key_projected, value_projected, mode_decay_speed, residue, out_weight):
    vmem, dma = pltpu.VMEM, pltpu.SemaphoreType.DMA
    units = len(UNITS)
    return pl.pallas_call(
        kernel,
        out_shape=jax.ShapeDtypeStruct((ROWS, COLS), BF16),
        in_specs=[pl.BlockSpec(memory_space=pl.ANY)] * 6,
        out_specs=pl.BlockSpec(memory_space=pl.ANY),
        scratch_shapes=[
            vmem((ROWS, WIDTH), BF16), vmem((ROWS, WIDTH), BF16), vmem((ROWS, WIDTH), BF16),
            vmem((WIDTH, 16), F32), vmem((WIDTH, 16), F32), vmem((8, WIDTH, COLS), BF16),
            vmem((128, 128), F32), vmem((128, 128), F32), vmem((128, 128), F32),
            vmem((ROWS * 8, 128), F32), vmem((ROWS * 8, 128), F32),
            vmem((128, 128), F32), vmem((128, 128), F32), vmem((64, 128), F32), vmem((CHIPS, 64, 128), F32),
            vmem((128, 128), F32), vmem((ROWS, WIDTH), BF16), vmem((8, ROWS, COLS), F32),
            vmem((2, units, BLOCK, COLS), BF16), vmem((2, units, BLOCK, COLS), BF16), vmem((ROWS, COLS), BF16),
            dma((5,)), dma((8,)), dma((2,)), dma((2,)), dma((CHIPS,)), dma((CHIPS,)), dma((1,)), dma((1,)),
            dma((2, units)), dma((2, units)), dma((4,)),
        ],
        compiler_params=pltpu.CompilerParams(collective_id=0, has_side_effects=True, vmem_limit_bytes=48 << 20),
        name="hyena",
    )(query_proj, key_projected, value_projected, mode_decay_speed, residue, out_weight)


def solution(mesh):
    return jax.shard_map(
        per_device,
        mesh=mesh,
        in_specs=(P("seq", "ch"), P("seq", "ch"), P("seq", "ch"), P("ch", None), P("ch", None), P("ch", None)),
        out_specs=P("seq", "ch"),
        check_vma=False,
    )
```

```python
import jax
import jax.numpy as jnp
from jax import lax
from jax.experimental import pallas as pl
from jax.experimental.pallas import tpu as pltpu
from jax.sharding import PartitionSpec as P

MESH = pl.DeviceIdType.MESH
F32, BF16 = jnp.float32, jnp.bfloat16

ROWS = 256
WIDTH = 1024
COLS = 512
BLOCK = 64
SIDE = 4

HOPS = ((4, 4, 3, 3), (3, 3, 4, 4))
ORDER = (
    ((0, 0), (2, 0), (1, 0), (3, 0), (0, 1), (1, 1), (2, 1), (3, 1), (0, 2), (1, 2), (2, 2), (3, 2), (0, 3), (1, 3)),
    ((0, 0), (2, 0), (1, 0), (3, 0), (2, 1), (0, 1), (3, 1), (1, 1), (2, 2), (3, 2), (0, 2), (1, 2), (2, 3), (3, 3)),
)
UNITS = len(ORDER[0])
INDEX = tuple({unit: at for at, unit in enumerate(order)} for order in ORDER)


def relative(direction, block, step):
    left_over = HOPS[direction][block] - step
    return left_over if direction == 0 else 8 - left_over


def one_minus_exp(u):
    series = jnp.ones_like(u)
    for order in range(8, 1, -1):
        series = 1.0 - u * series * (1.0 / order)
    return jnp.where(u < 0.25, u * series, 1.0 - jnp.exp(-u))


def kernel(
    q_hbm, k_hbm, v_hbm, decay_hbm, residue_hbm, w_hbm, out,
    q_buf, k_buf, v_buf, decay_buf, residue_buf, w_buf,
    rate, ratio, weight, xs, ys, own, other, total, row_total, totals, carry, gated, part, sent, received,
    load_sem, w_sem, core_send, core_recv, total_send, total_recv, carry_send, carry_recv, z_send, z_recv,
):
    seq, z = lax.axis_index("seq"), lax.axis_index("ch")
    chip, core = lax.div(seq, 2), lax.rem(seq, 2)
    at_x, at_y = lax.div(chip, SIDE), lax.rem(chip, SIDE)
    is_second = core == 1

    def device(x, y, core_at):
        return {"seq": (x * SIDE + y) * 2 + core_at, "ch": z}

    def z_neighbour(direction):
        return {"seq": seq, "ch": lax.rem(z + (1 if direction == 0 else 7), 8)}

    other_core = device(at_x, at_y, 1 - core)

    barrier = pltpu.get_barrier_semaphore()
    for d in range(1, SIDE):
        for partner in (device(lax.rem(at_x + d, SIDE), at_y, core), device(at_x, lax.rem(at_y + d, SIDE), core)):
            pl.semaphore_signal(barrier, inc=1, device_id=partner, device_id_type=MESH)
    for partner in (other_core, z_neighbour(0), z_neighbour(1)):
        pl.semaphore_signal(barrier, inc=1, device_id=partner, device_id_type=MESH)

    loads = [
        pltpu.make_async_copy(source, target, load_sem.at[at])
        for at, (source, target) in enumerate(
            [(decay_hbm, decay_buf), (k_hbm, k_buf), (v_hbm, v_buf), (residue_hbm, residue_buf), (q_hbm, q_buf)]
        )
    ]
    for load in loads:
        load.start()

    loads[0].wait()
    for j in range(8):
        rate[pl.ds(j, 16, stride=8), :] = decay_buf[:, pl.ds(128 * j, 128)]
    ratio[...] = jnp.exp(-rate[...])

    loads[1].wait()
    loads[2].wait()
    w_loads = {}
    for rd in (4, 5, 3, 2, 6, 1, 7, 0):
        columns = pl.ds(pl.multiple_of(lax.rem(z + rd, 8) * COLS, COLS), COLS)
        w_loads[rd] = pltpu.make_async_copy(w_hbm.at[:, columns], w_buf.at[rd], w_sem.at[rd])
        w_loads[rd].start()

    def carrier_rows(i, _):
        rows = pl.ds(pl.multiple_of(i * 16, 16), 16)
        product = (k_buf[rows, :].astype(F32) * v_buf[rows, :].astype(F32)).astype(BF16).astype(F32)
        for j in range(8):
            xs[pl.ds(i * 128 + j, 16, stride=8), :] = product[:, 128 * j : 128 * j + 128]
        return 0

    lax.fori_loop(0, ROWS // 16, carrier_rows, 0)

    def row(ref, t):
        return ref[pl.ds(pl.multiple_of(t * 8, 8), 8), :]

    def modes(ref, half):
        return [row(ref, half * 8 + n) for n in range(8)]

    def own_state(half):
        a = modes(ratio, half)
        a4 = [(s * s) * (s * s) for s in a]

        def four(i, state):
            x = [row(xs, 4 * i + r) for r in range(4)]
            return tuple(a4[n] * state[n] + (((a[n] * x[0] + x[1]) * a[n] + x[2]) * a[n] + x[3]) for n in range(8))

        state = lax.fori_loop(0, ROWS // 4, four, tuple(jnp.zeros((8, 128), F32) for _ in range(8)))
        for n in range(8):
            own[pl.ds(pl.multiple_of((half * 8 + n) * 8, 8), 8), :] = state[n]

    def half_rows(half):
        return pl.ds(pl.multiple_of(half * 64, 64), 64)

    mine, theirs = half_rows(core), half_rows(1 - core)

    def core_copy(half, at):
        return pltpu.make_async_remote_copy(
            src_ref=own.at[half_rows(half), :], dst_ref=other.at[half_rows(half), :],
            send_sem=core_send.at[at], recv_sem=core_recv.at[at], device_id=other_core, device_id_type=MESH,
        )

    own_state(1 - core)
    pl.semaphore_wait(barrier, 2 * (SIDE - 1) + 3)
    first = core_copy(1 - core, 0)
    first.start()
    own_state(core)
    second = core_copy(core, 1)
    second.start()

    device_decay = jnp.exp(rate[mine, :] * -float(ROWS))
    chip_decay = jnp.exp(rate[mine, :] * -float(2 * ROWS))
    first.wait_recv()
    older = jnp.where(is_second, other[mine, :], own[mine, :])
    newer = jnp.where(is_second, own[mine, :], other[mine, :])
    total[...] = (device_decay * older + newer).astype(BF16)

    def y_copy(d):
        return pltpu.make_async_remote_copy(
            src_ref=total, dst_ref=totals.at[at_y], send_sem=total_send.at[d], recv_sem=total_recv.at[at_y],
            device_id=device(at_x, lax.rem(at_y + d, SIDE), core), device_id_type=MESH,
        )

    def x_copies(act):
        for d in range(SIDE - 1, 0, -1):
            @pl.when(at_x + d < SIDE)
            def _():
                act(pltpu.make_async_remote_copy(
                    src_ref=row_total, dst_ref=totals.at[SIDE + at_x],
                    send_sem=total_send.at[SIDE + d], recv_sem=total_recv.at[SIDE + at_x],
                    device_id=device(at_x + d, at_y, core), device_id_type=MESH,
                ))

    def landed(at):
        return pltpu.make_async_remote_copy(
            src_ref=total, dst_ref=totals.at[at], send_sem=total_send.at[0], recv_sem=total_recv.at[at],
            device_id=other_core, device_id_type=MESH,
        )

    for d in (2, 3, 1):
        y_copy(d).start()
    totals[at_y] = total[...]

    loads[3].wait()
    for j in range(8):
        weight[pl.ds(j, 16, stride=8), :] = residue_buf[:, pl.ds(128 * j, 128)]
    weight[...] = weight[...] * jnp.sqrt(one_minus_exp(2.0 * rate[...]))

    def local(half):
        a, w = modes(ratio, half), modes(weight, half)

        def four(i, state):
            for r in range(4):
                t = 4 * i + r
                x = row(xs, t)
                state = tuple(a[n] * state[n] + x for n in range(8))
                terms = [w[n] * state[n] for n in range(8)]
                y = ((terms[0] + terms[1]) + (terms[2] + terms[3])) + ((terms[4] + terms[5]) + (terms[6] + terms[7]))
                if half == 1:
                    y = y + row(ys, t)
                ys[pl.ds(pl.multiple_of(t * 8, 8), 8), :] = y
            return state

        lax.fori_loop(0, ROWS // 4, four, tuple(jnp.zeros((8, 128), F32) for _ in range(8)))

    local(0)

    for d in (1, 3, 2):
        landed(lax.rem(at_y + d, SIDE)).wait_recv()
    whole = partial = jnp.zeros((64, 128), F32)
    for y in range(SIDE):
        value = totals[y].astype(F32)
        whole = chip_decay * whole + value
        partial = jnp.where(y < at_y, chip_decay * partial + value, partial)
    row_total[...] = whole.astype(BF16)
    x_copies(lambda copy: copy.start())
    local(1)

    row_decay = jnp.exp(rate[mine, :] * -float(2 * SIDE * ROWS))

    def add_row(x, state):
        landed(SIDE + x).wait_recv()
        return row_decay * state + totals[SIDE + x].astype(F32)

    rows_before = lax.fori_loop(0, at_x, add_row, jnp.zeros((64, 128), F32))
    carry[mine, :] = jnp.exp(rate[mine, :] * (-float(2 * ROWS) * at_y.astype(F32))) * rows_before + partial
    carry_copy = pltpu.make_async_remote_copy(
        src_ref=carry.at[mine, :], dst_ref=carry.at[mine, :], send_sem=carry_send.at[0], recv_sem=carry_recv.at[0],
        device_id=other_core, device_id_type=MESH,
    )
    carry_copy.start()

    def weighted(rows):
        before = jnp.exp(rate[rows, :] * -float(ROWS)) * carry[rows, :] + other[rows, :]
        return weight[rows, :] * jnp.where(is_second, before, carry[rows, :])

    def add_carried(half, start, first_row, count):
        a = modes(ratio, half)

        def four(i, state):
            for r in range(4):
                t = first_row + 4 * i + r
                state = tuple(a[n] * state[n] for n in range(8))
                sums = [(state[4 * m] + state[4 * m + 1]) + (state[4 * m + 2] + state[4 * m + 3]) for m in range(2)]
                ys[pl.ds(pl.multiple_of(t * 8, 8), 8), :] = row(ys, t) + (sums[0] + sums[1])
            return state

        lax.fori_loop(0, count // 4, four, tuple(start[8 * n : 8 * n + 8] for n in range(8)))

    add_carried(core, weighted(mine), 0, ROWS)
    second.wait_recv()
    loads[4].wait()
    carry_copy.wait_recv()
    own_carry = weighted(theirs)

    def gate(block):
        add_carried(1 - core, own_carry * jnp.exp(rate[theirs, :] * -float(block * BLOCK)), block * BLOCK, BLOCK)

        def sixteen(i, _):
            rows = pl.ds(pl.multiple_of(block * BLOCK + i * 16, 16), 16)
            for j in range(8):
                lanes = pl.ds(128 * j, 128)
                y = ys[pl.ds((block * BLOCK + i * 16) * 8 + j, 16, stride=8), :]
                gated[rows, lanes] = (q_buf[rows, lanes].astype(F32) * y).astype(BF16)
            return 0

        lax.fori_loop(0, BLOCK // 16, sixteen, 0)

    def rows_of(block):
        return pl.ds(block * BLOCK, BLOCK)

    def z_copy(direction, at):
        return pltpu.make_async_remote_copy(
            src_ref=sent.at[direction, at], dst_ref=received.at[direction, at],
            send_sem=z_send.at[direction, at], recv_sem=z_recv.at[direction, at],
            device_id=z_neighbour(direction), device_id_type=MESH,
        )

    for rd in (4, 5, 3):
        w_loads[rd].wait()
    for at in range(4):
        block = ORDER[0][at][0]
        gate(block)
        for direction in range(2):
            product = jnp.dot(gated[rows_of(block), :], w_buf[relative(direction, block, 0)], preferred_element_type=F32)
            sent[direction, at] = product.astype(BF16)
            z_copy(direction, at).start()

    def products(k, _):
        rd = jnp.where(lax.rem(k, 2) == 0, 3 - lax.div(k, 2), 5 + lax.div(k, 2))
        for n in range(2):
            lanes = pl.ds(256 * n, 256)
            part[rd, :, lanes] = jnp.dot(gated[...], w_buf[rd, :, lanes], preferred_element_type=F32)
        return 0

    for rd in (2, 6):
        w_loads[rd].wait()
    lax.fori_loop(0, 4, products, 0)

    for at in range(4, UNITS):
        if at == 8:
            for rd in (1, 7, 0):
                w_loads[rd].wait()
            lax.fori_loop(4, 7, products, 0)
        for direction in range(2):
            block, step = ORDER[direction][at]
            previous = INDEX[direction][block, step - 1]
            z_copy(direction, previous).wait_recv()
            summed = part[relative(direction, block, step), rows_of(block), :] + received[direction, previous].astype(F32)
            sent[direction, at] = summed.astype(BF16)
            z_copy(direction, at).start()

    for block in (0, 2, 1, 3):
        summed = part[0, rows_of(block), :]
        for direction in range(2):
            last = INDEX[direction][block, HOPS[direction][block] - 1]
            z_copy(direction, last).wait_recv()
            summed = summed + received[direction, last].astype(F32)
        out[rows_of(block), :] = summed.astype(BF16)

    first.wait_send()
    second.wait_send()
    for d in range(1, SIDE):
        y_copy(d).wait_send()
    x_copies(lambda copy: copy.wait_send())
    carry_copy.wait_send()
    for direction in range(2):
        for at in range(UNITS):
            z_copy(direction, at).wait_send()


def per_device(query_proj, key_projected, value_projected, mode_decay_speed, residue, out_weight):
    vmem, dma = pltpu.VMEM, pltpu.SemaphoreType.DMA
    operands = (query_proj, key_projected, value_projected, mode_decay_speed.T, residue.T, out_weight)
    return pl.pallas_call(
        kernel,
        out_shape=jax.ShapeDtypeStruct((ROWS, COLS), BF16),
        in_specs=[pl.BlockSpec(memory_space=pltpu.HBM)] * 6,
        out_specs=pl.BlockSpec(memory_space=pltpu.VMEM),
        scratch_shapes=[
            vmem((ROWS, WIDTH), BF16), vmem((ROWS, WIDTH), BF16), vmem((ROWS, WIDTH), BF16),
            vmem((16, WIDTH), F32), vmem((16, WIDTH), F32), vmem((8, WIDTH, COLS), BF16),
            vmem((128, 128), F32), vmem((128, 128), F32), vmem((128, 128), F32),
            vmem((ROWS * 8, 128), F32), vmem((ROWS * 8, 128), F32),
            vmem((128, 128), F32), vmem((128, 128), F32),
            vmem((64, 128), BF16), vmem((64, 128), BF16), vmem((2 * SIDE, 64, 128), BF16),
            vmem((128, 128), F32), vmem((ROWS, WIDTH), BF16), vmem((8, ROWS, COLS), F32),
            vmem((2, UNITS, BLOCK, COLS), BF16), vmem((2, UNITS, BLOCK, COLS), BF16),
            dma((5,)), dma((8,)), dma((2,)), dma((2,)), dma((2 * SIDE,)), dma((2 * SIDE,)), dma((1,)), dma((1,)),
            dma((2, UNITS)), dma((2, UNITS)),
        ],
        compiler_params=pltpu.CompilerParams(collective_id=0, has_side_effects=True, vmem_limit_bytes=48 << 20),
        name="hyena",
    )(*(pltpu.with_memory_space_constraint(operand, pltpu.HBM) for operand in operands))


def solution(mesh):
    return jax.shard_map(
        per_device,
        mesh=mesh,
        in_specs=(P("seq", "ch"), P("seq", "ch"), P("seq", "ch"), P("ch", None), P("ch", None), P("ch", None)),
        out_specs=P("seq", "ch"),
        check_vma=False,
    )
```

```python
import jax
import jax.numpy as jnp
from jax import lax
from jax.experimental import pallas as pl
from jax.experimental.pallas import tpu as pltpu
from jax.sharding import PartitionSpec as P

MESH = pl.DeviceIdType.MESH
F32, BF16 = jnp.float32, jnp.bfloat16

ROWS = 256
WIDTH = 1024
COLS = 512
BLOCK = 64
STEP = 8
SIDE = 4

HOPS = ((4, 4, 3, 3), (3, 3, 4, 4))
ORDER = (
    ((0, 0), (2, 0), (1, 0), (3, 0), (0, 1), (1, 1), (2, 1), (3, 1), (0, 2), (1, 2), (2, 2), (3, 2), (0, 3), (1, 3)),
    ((0, 0), (2, 0), (1, 0), (3, 0), (2, 1), (0, 1), (3, 1), (1, 1), (2, 2), (3, 2), (0, 2), (1, 2), (2, 3), (3, 3)),
)
UNITS = len(ORDER[0])
INDEX = tuple({unit: at for at, unit in enumerate(order)} for order in ORDER)


def relative(direction, block, step):
    left_over = HOPS[direction][block] - step
    return left_over if direction == 0 else 8 - left_over


def one_minus_exp(u):
    series = jnp.ones_like(u)
    for order in range(8, 1, -1):
        series = 1.0 - u * series * (1.0 / order)
    return jnp.where(u < 0.25, u * series, 1.0 - jnp.exp(-u))


def kernel(
    q_hbm, k_hbm, v_hbm, decay_hbm, residue_hbm, w_hbm, out,
    q_buf, k_buf, v_buf, decay_buf, residue_buf, w_buf,
    rate, ratio, ratio_step, weight, decays, starts, taps, kept, xs, ys, own, states, row_total, row_totals, prefixes, before, sent_before, gated, part, sent, received,
    load_sem, w_sem, state_send, state_recv, row_send, row_recv, core_send, core_recv, z_send, z_recv,
):
    seq, z = lax.axis_index("seq"), lax.axis_index("ch")
    chip, core = lax.div(seq, 2), lax.rem(seq, 2)
    at_x, at_y = lax.div(chip, SIDE), lax.rem(chip, SIDE)
    is_second = core == 1

    def device(x, y, core_at):
        return {"seq": (x * SIDE + y) * 2 + core_at, "ch": z}

    def z_neighbour(direction):
        return {"seq": seq, "ch": lax.rem(z + (1 if direction == 0 else 7), 8)}

    other_core = device(at_x, at_y, 1 - core)

    loads = [
        pltpu.make_async_copy(source, target, load_sem.at[at])
        for at, (source, target) in enumerate(
            [(decay_hbm, decay_buf), (k_hbm, k_buf), (v_hbm, v_buf), (residue_hbm, residue_buf), (q_hbm, q_buf)]
        )
    ]
    for load in loads:
        load.start()

    barrier = pltpu.get_barrier_semaphore()
    def greet(partner):
        pl.semaphore_signal(barrier, inc=1, device_id=partner, device_id_type=MESH)

    greet(other_core)
    greet(z_neighbour(0))
    greet(z_neighbour(1))

    @pl.when(is_second)
    def _():
        for d in range(1, SIDE):
            near = lax.rem(at_y + d, SIDE)
            for partner in (device(lax.rem(at_x + d, SIDE), at_y, 1), device(at_x, near, 1), device(at_x, near, 0)):
                greet(partner)

    loads[0].wait()
    for j in range(8):
        rate[pl.ds(j, 16, stride=8), :] = decay_buf[:, pl.ds(128 * j, 128)]
    ratio[...] = jnp.exp(-rate[...])
    ratio_step[...] = jnp.exp(-float(STEP) * rate[...])

    loads[1].wait()
    loads[2].wait()
    w_loads = {}
    for rd in (4, 5, 3, 2, 6, 1, 7, 0):
        columns = pl.ds(pl.multiple_of(lax.rem(z + rd, 8) * COLS, COLS), COLS)
        w_loads[rd] = pltpu.make_async_copy(w_hbm.at[:, columns], w_buf.at[rd], w_sem.at[rd])
        w_loads[rd].start()

    def carrier_rows(i, _):
        rows = pl.ds(pl.multiple_of(i * 16, 16), 16)
        product = (k_buf[rows, :].astype(F32) * v_buf[rows, :].astype(F32)).astype(BF16).astype(F32)
        for j in range(8):
            xs[pl.ds(i * 128 + j, 16, stride=8), :] = product[:, 128 * j : 128 * j + 128]
        return 0

    lax.fori_loop(0, ROWS // 16, carrier_rows, 0)

    def row(ref, t):
        return ref[pl.ds(pl.multiple_of(t * 8, 8), 8), :]

    def modes(ref, half):
        return [row(ref, half * 8 + n) for n in range(8)]

    def own_state(half):
        a, a_step = modes(ratio, half), modes(ratio_step, half)

        def step(i, state):
            x = [row(xs, STEP * i + r) for r in range(STEP)]
            after = []
            for n in range(8):
                kept[pl.ds(pl.multiple_of((i * 16 + half * 8 + n) * 8, 8), 8), :] = state[n]
                added = x[0]
                for r in range(1, STEP):
                    added = added * a[n] + x[r]
                after.append(a_step[n] * state[n] + added)
            return tuple(after)

        state = lax.fori_loop(0, ROWS // STEP, step, tuple(jnp.zeros((8, 128), F32) for _ in range(8)))
        own[half] = jnp.concatenate(state, axis=0).astype(BF16)

    def state_copy(half, d):
        return pltpu.make_async_remote_copy(
            src_ref=own.at[half], dst_ref=states.at[2 * at_y + core, half],
            send_sem=state_send.at[half, d], recv_sem=state_recv.at[2 * at_y + core, half],
            device_id=device(at_x, lax.rem(at_y + d, SIDE), 1), device_id_type=MESH,
        )

    def state_copies(half, act):
        for d in (2, 3, 1):
            act(state_copy(half, d))

        @pl.when(jnp.logical_not(is_second))
        def _():
            act(state_copy(half, 0))

    own_state(0)
    @pl.when(is_second)
    def _():
        pl.semaphore_wait(barrier, 3 * (SIDE - 1))

    @pl.when(jnp.logical_not(is_second))
    def _():
        pl.semaphore_wait(barrier, SIDE + 2)

    state_copies(0, lambda copy: copy.start())
    own_state(1)
    state_copies(1, lambda copy: copy.start())

    def row_copies(half, act):
        for d in range(SIDE - 1, 0, -1):
            @pl.when(at_x + d < SIDE)
            def _():
                act(pltpu.make_async_remote_copy(
                    src_ref=row_total.at[half], dst_ref=row_totals.at[at_x, half],
                    send_sem=row_send.at[d, half], recv_sem=row_recv.at[at_x, half],
                    device_id=device(at_x + d, at_y, 1), device_id_type=MESH,
                ))

    loads[3].wait()
    for j in range(8):
        weight[pl.ds(j, 16, stride=8), :] = residue_buf[:, pl.ds(128 * j, 128)]
    weight[...] = weight[...] * jnp.sqrt(one_minus_exp(2.0 * rate[...]))
    decays[0] = jnp.exp(-float(ROWS) * rate[...])
    decays[1] = jnp.exp(-float(2 * SIDE * ROWS) * rate[...])
    for core_at in range(2):
        decays[2 + core_at] = jnp.exp(rate[...] * (-float(ROWS) * (2 * at_y + core_at).astype(F32)))
    for block in range(ROWS // BLOCK):
        starts[block] = weight[...] * jnp.exp(rate[...] * -float(block * BLOCK))

    power = weight[...]
    for k in range(STEP):
        tap = power[0:8]
        for n in range(1, 16):
            tap = tap + power[8 * n : 8 * n + 8]
        taps[8 * k : 8 * k + 8, :] = tap
        power = power * ratio[...]

    def local(i, _):
        f = [row(taps, k) for k in range(STEP)]
        x = [row(xs, STEP * i + r) for r in range(STEP)]
        for r in range(STEP):
            y = f[r] * x[0]
            for k in range(1, r + 1):
                y = y + f[r - k] * x[k]
            ys[pl.ds(pl.multiple_of((STEP * i + r) * 8, 8), 8), :] = y
        rows = pl.ds(pl.multiple_of(i * 128, 128), 128)
        kept[rows, :] = kept[rows, :] * weight[...]
        return 0

    lax.fori_loop(0, ROWS // STEP, local, 0)

    @pl.when(is_second)
    def _():
        states[2 * at_y + 1, 0] = own[0]
        states[2 * at_y + 1, 1] = own[1]
        prefixes[0] = jnp.zeros((128, 128), F32)

        def wait_state(i, _):
            sender = lax.rem(2 * at_y + 2 + i, 2 * SIDE)
            for half in range(2):
                pltpu.make_async_remote_copy(
                    src_ref=own.at[half], dst_ref=states.at[sender, half], send_sem=state_send.at[half, 0],
                    recv_sem=state_recv.at[sender, half], device_id=other_core, device_id_type=MESH,
                ).wait_recv()
            return 0

        lax.fori_loop(0, 2 * SIDE - 1, wait_state, 0)
        for half in range(2):
            rows = pl.ds(64 * half, 64)
            device_decay = decays[0, rows, :]
            whole = states[0, half].astype(F32)
            for at in range(1, 2 * SIDE):
                prefixes[at, rows, :] = whole
                whole = device_decay * whole + states[at, half].astype(F32)
            row_total[half] = whole.astype(BF16)
            row_copies(half, lambda copy: copy.start())

    def core_copy(half):
        return pltpu.make_async_remote_copy(
            src_ref=sent_before.at[half], dst_ref=before.at[half], send_sem=core_send.at[half], recv_sem=core_recv.at[half],
            device_id=other_core, device_id_type=MESH,
        )

    @pl.when(is_second)
    def _():
        for half in range(2):
            rows = pl.ds(64 * half, 64)
            row_decay = decays[1, rows, :]

            def add_row(x, state):
                pltpu.make_async_remote_copy(
                    src_ref=row_total.at[half], dst_ref=row_totals.at[x, half], send_sem=row_send.at[0, half],
                    recv_sem=row_recv.at[x, half], device_id=other_core, device_id_type=MESH,
                ).wait_recv()
                return row_decay * state + row_totals[x, half].astype(F32)

            rows_before = lax.fori_loop(0, at_x, add_row, jnp.zeros((64, 128), F32))
            sent_before[half] = decays[2, rows, :] * rows_before + prefixes[2 * at_y, rows, :]
            core_copy(half).start()
            before[half] = decays[3, rows, :] * rows_before + prefixes[2 * at_y + 1, rows, :]

    @pl.when(jnp.logical_not(is_second))
    def _():
        core_copy(0).wait_recv()
        core_copy(1).wait_recv()

    loads[4].wait()
    def gate(block):
        a = modes(ratio, 0) + modes(ratio, 1)

        def step(i, carried):
            at = block * (BLOCK // STEP) + i
            state = tuple(carried[n] + row(kept, at * 16 + n) for n in range(16))
            for r in range(STEP):
                t = STEP * at + r
                state = tuple(a[n] * state[n] for n in range(16))
                sums = [(state[4 * m] + state[4 * m + 1]) + (state[4 * m + 2] + state[4 * m + 3]) for m in range(4)]
                ys[pl.ds(pl.multiple_of(t * 8, 8), 8), :] = row(ys, t) + ((sums[0] + sums[1]) + (sums[2] + sums[3]))
            return tuple(carried[n] * row(ratio_step, n) for n in range(16))

        lax.fori_loop(0, BLOCK // STEP, step, tuple(
            before[n // 8, 8 * (n % 8) : 8 * (n % 8) + 8, :] * starts[block, 8 * n : 8 * n + 8, :] for n in range(16)
        ))

        def sixteen(i, _):
            rows = pl.ds(pl.multiple_of(block * BLOCK + i * 16, 16), 16)
            for j in range(8):
                lanes = pl.ds(128 * j, 128)
                y = ys[pl.ds((block * BLOCK + i * 16) * 8 + j, 16, stride=8), :]
                gated[rows, lanes] = (q_buf[rows, lanes].astype(F32) * y).astype(BF16)
            return 0

        lax.fori_loop(0, BLOCK // 16, sixteen, 0)

    def rows_of(block):
        return pl.ds(block * BLOCK, BLOCK)

    def z_copy(direction, at):
        return pltpu.make_async_remote_copy(
            src_ref=sent.at[direction, at], dst_ref=received.at[direction, at],
            send_sem=z_send.at[direction, at], recv_sem=z_recv.at[direction, at],
            device_id=z_neighbour(direction), device_id_type=MESH,
        )

    for rd in (4, 5, 3):
        w_loads[rd].wait()
    for at in range(4):
        block = ORDER[0][at][0]
        gate(block)
        for direction in range(2):
            product = jnp.dot(gated[rows_of(block), :], w_buf[relative(direction, block, 0)], preferred_element_type=F32)
            sent[direction, at] = product.astype(BF16)
            z_copy(direction, at).start()

    def products(k, _):
        rd = jnp.where(lax.rem(k, 2) == 0, 3 - lax.div(k, 2), 5 + lax.div(k, 2))
        for n in range(2):
            lanes = pl.ds(256 * n, 256)
            part[rd, :, lanes] = jnp.dot(gated[...], w_buf[rd, :, lanes], preferred_element_type=F32)
        return 0

    for rd in (2, 6):
        w_loads[rd].wait()
    lax.fori_loop(0, 4, products, 0)

    for at in range(4, UNITS):
        if at == 8:
            for rd in (1, 7, 0):
                w_loads[rd].wait()
            lax.fori_loop(4, 7, products, 0)
        for direction in range(2):
            block, step = ORDER[direction][at]
            previous = INDEX[direction][block, step - 1]
            z_copy(direction, previous).wait_recv()
            summed = part[relative(direction, block, step), rows_of(block), :] + received[direction, previous].astype(F32)
            sent[direction, at] = summed.astype(BF16)
            z_copy(direction, at).start()

    for block in (0, 2, 1, 3):
        summed = part[0, rows_of(block), :]
        for direction in range(2):
            last = INDEX[direction][block, HOPS[direction][block] - 1]
            z_copy(direction, last).wait_recv()
            summed = summed + received[direction, last].astype(F32)
        out[rows_of(block), :] = summed.astype(BF16)

    state_copies(0, lambda copy: copy.wait_send())
    state_copies(1, lambda copy: copy.wait_send())

    @pl.when(is_second)
    def _():
        for half in range(2):
            row_copies(half, lambda copy: copy.wait_send())
            core_copy(half).wait_send()

    for direction in range(2):
        for at in range(UNITS):
            z_copy(direction, at).wait_send()


def per_device(query_proj, key_projected, value_projected, mode_decay_speed, residue, out_weight):
    vmem, dma = pltpu.VMEM, pltpu.SemaphoreType.DMA
    operands = (query_proj, key_projected, value_projected, mode_decay_speed.T, residue.T, out_weight)
    return pl.pallas_call(
        kernel,
        out_shape=jax.ShapeDtypeStruct((ROWS, COLS), BF16),
        in_specs=[pl.BlockSpec(memory_space=pltpu.HBM)] * 6,
        out_specs=pl.BlockSpec(memory_space=pltpu.VMEM),
        scratch_shapes=[
            vmem((ROWS, WIDTH), BF16), vmem((ROWS, WIDTH), BF16), vmem((ROWS, WIDTH), BF16),
            vmem((16, WIDTH), F32), vmem((16, WIDTH), F32), vmem((8, WIDTH, COLS), BF16),
            vmem((128, 128), F32), vmem((128, 128), F32), vmem((128, 128), F32), vmem((128, 128), F32),
            vmem((4, 128, 128), F32), vmem((ROWS // BLOCK, 128, 128), F32), vmem((STEP * 8, 128), F32), vmem((ROWS // STEP * 128, 128), F32), vmem((ROWS * 8, 128), F32), vmem((ROWS * 8, 128), F32),
            vmem((2, 64, 128), BF16), vmem((2 * SIDE, 2, 64, 128), BF16), vmem((2, 64, 128), BF16), vmem((SIDE, 2, 64, 128), BF16),
            vmem((2 * SIDE, 128, 128), F32), vmem((2, 64, 128), F32), vmem((2, 64, 128), F32), vmem((ROWS, WIDTH), BF16), vmem((8, ROWS, COLS), F32),
            vmem((2, UNITS, BLOCK, COLS), BF16), vmem((2, UNITS, BLOCK, COLS), BF16),
            dma((5,)), dma((8,)), dma((2, SIDE)), dma((2 * SIDE, 2)), dma((SIDE, 2)), dma((SIDE, 2)), dma((2,)), dma((2,)),
            dma((2, UNITS)), dma((2, UNITS)),
        ],
        compiler_params=pltpu.CompilerParams(collective_id=0, has_side_effects=True, vmem_limit_bytes=48 << 20),
        name="hyena",
    )(*(pltpu.with_memory_space_constraint(operand, pltpu.HBM) for operand in operands))


def solution(mesh):
    return jax.shard_map(
        per_device,
        mesh=mesh,
        in_specs=(P("seq", "ch"), P("seq", "ch"), P("seq", "ch"), P("ch", None), P("ch", None), P("ch", None)),
        out_specs=P("seq", "ch"),
        check_vma=False,
    )
```

```python
import jax
import jax.numpy as jnp
from jax import lax
from jax.experimental import pallas as pl
from jax.experimental.pallas import tpu as pltpu
from jax.sharding import PartitionSpec as P

MESH = pl.DeviceIdType.MESH
F32, BF16 = jnp.float32, jnp.bfloat16

ROWS = 256
WIDTH = 1024
COLS = 512
BLOCK = 64
STEP = 8
SIDE = 4

HOPS = ((4, 4, 3, 3), (3, 3, 4, 4))
ORDER = (
    ((0, 0), (2, 0), (1, 0), (3, 0), (0, 1), (1, 1), (2, 1), (3, 1), (0, 2), (1, 2), (2, 2), (3, 2), (0, 3), (1, 3)),
    ((0, 0), (2, 0), (1, 0), (3, 0), (2, 1), (1, 1), (3, 1), (0, 1), (2, 2), (3, 2), (1, 2), (0, 2), (2, 3), (3, 3)),
)
UNITS = len(ORDER[0])
TURNED = (5, 6, 7)
INDEX = tuple({unit: at for at, unit in enumerate(order)} for order in ORDER)


def relative(direction, block, step):
    left_over = HOPS[direction][block] - step
    return left_over if direction == 0 else 8 - left_over


def one_minus_exp(u):
    series = jnp.ones_like(u)
    for order in range(8, 1, -1):
        series = 1.0 - u * series * (1.0 / order)
    return jnp.where(u < 0.25, u * series, 1.0 - jnp.exp(-u))


def kernel(
    q_hbm, k_hbm, v_hbm, decay_hbm, residue_hbm, w_hbm, out,
    q_buf, k_buf, v_buf, decay_buf, residue_buf, w_buf,
    rate, ratio, ratio_step, weight, decays, starts, taps, kept, xs, ys, own, states, row_total, row_totals, prefixes, before, sent_before, gated, part, sent, received, turned,
    load_sem, w_sem, state_send, state_recv, row_ready, row_send, row_recv, core_send, core_recv, z_send, z_recv, turned_send, turned_recv,
):
    seq, z = lax.axis_index("seq"), lax.axis_index("ch")
    chip, core = lax.div(seq, 2), lax.rem(seq, 2)
    at_x, at_y = lax.div(chip, SIDE), lax.rem(chip, SIDE)
    is_second = core == 1

    def any_of(places):
        found = z == places[0]
        for place in places[1:]:
            found = found | (z == place)
        return found

    is_from = any_of(TURNED)
    is_via = any_of([place - 1 for place in TURNED])
    is_spared = any_of([(place + 1) % 8 for place in TURNED])

    def device(x, y, core_at):
        return {"seq": (x * SIDE + y) * 2 + core_at, "ch": z}

    def z_neighbour(direction):
        return {"seq": seq, "ch": lax.rem(z + (1 if direction == 0 else 7), 8)}

    other_core = device(at_x, at_y, 1 - core)

    loads = [
        pltpu.make_async_copy(source, target, load_sem.at[at])
        for at, (source, target) in enumerate(
            [(decay_hbm, decay_buf), (k_hbm, k_buf), (v_hbm, v_buf), (residue_hbm, residue_buf), (q_hbm, q_buf)]
        )
    ]
    for load in loads:
        load.start()

    barrier = pltpu.get_barrier_semaphore()
    def greet(partner):
        pl.semaphore_signal(barrier, inc=1, device_id=partner, device_id_type=MESH)

    greet(other_core)
    greet(z_neighbour(0))
    greet(z_neighbour(1))

    @pl.when(is_second)
    def _():
        for d in (2, 1, 3):
            near = lax.rem(at_y + d, SIDE)
            for partner in (device(at_x, near, 1), device(at_x, near, 0)):
                greet(partner)

        for d in range(1, SIDE):
            @pl.when(at_x + d < SIDE)
            def _():
                greet(device(at_x + d, at_y, 1))

    loads[0].wait()
    for j in range(8):
        rate[pl.ds(j, 16, stride=8), :] = decay_buf[:, pl.ds(128 * j, 128)]
    ratio[...] = jnp.exp(-rate[...])
    ratio_step[...] = jnp.exp(-float(STEP) * rate[...])

    loads[1].wait()
    loads[2].wait()
    w_loads = {}
    for rd in (4, 5, 3, 2, 6, 1, 7, 0):
        columns = pl.ds(pl.multiple_of(lax.rem(z + rd, 8) * COLS, COLS), COLS)
        w_loads[rd] = pltpu.make_async_copy(w_hbm.at[:, columns], w_buf.at[rd], w_sem.at[rd])
        w_loads[rd].start()

    def carrier_rows(i, _):
        rows = pl.ds(pl.multiple_of(i * 16, 16), 16)
        product = (k_buf[rows, :].astype(F32) * v_buf[rows, :].astype(F32)).astype(BF16).astype(F32)
        for j in range(8):
            xs[pl.ds(i * 128 + j, 16, stride=8), :] = product[:, 128 * j : 128 * j + 128]
        return 0

    lax.fori_loop(0, ROWS // 16, carrier_rows, 0)

    def row(ref, t):
        return ref[pl.ds(pl.multiple_of(t * 8, 8), 8), :]

    def modes(ref, half):
        return [row(ref, half * 8 + n) for n in range(8)]

    def own_state(half):
        a, a_step = modes(ratio, half), modes(ratio_step, half)

        def step(i, state):
            x = [row(xs, STEP * i + r) for r in range(STEP)]
            after = []
            for n in range(8):
                kept[pl.ds(pl.multiple_of((i * 16 + half * 8 + n) * 8, 8), 8), :] = state[n]
                added = x[0]
                for r in range(1, STEP):
                    added = added * a[n] + x[r]
                after.append(a_step[n] * state[n] + added)
            return tuple(after)

        state = lax.fori_loop(0, ROWS // STEP, step, tuple(jnp.zeros((8, 128), F32) for _ in range(8)))
        own[half] = jnp.concatenate(state, axis=0).astype(BF16)

    def state_copy(half, d):
        return pltpu.make_async_remote_copy(
            src_ref=own.at[half], dst_ref=states.at[2 * at_y + core, half],
            send_sem=state_send.at[half, d], recv_sem=state_recv.at[2 * at_y + core, half],
            device_id=device(at_x, lax.rem(at_y + d, SIDE), 1), device_id_type=MESH,
        )

    def state_copies(half, act):
        for d in (2, 3, 1):
            act(state_copy(half, d))

        @pl.when(jnp.logical_not(is_second))
        def _():
            act(state_copy(half, 0))

    own_state(0)
    @pl.when(is_second)
    def _():
        pl.semaphore_wait(barrier, SIDE - 1 + 3 + at_x)
        for d in range(1, SIDE):
            @pl.when(at_x >= d)
            def _():
                pl.semaphore_signal(row_ready, inc=1, device_id=device(at_x - d, at_y, 1), device_id_type=MESH)

    @pl.when(jnp.logical_not(is_second))
    def _():
        pl.semaphore_wait(barrier, SIDE + 2)

    state_copies(0, lambda copy: copy.start())
    own_state(1)
    state_copies(1, lambda copy: copy.start())

    def row_copies(half, act):
        for d in range(SIDE - 1, 0, -1):
            @pl.when(at_x + d < SIDE)
            def _():
                act(pltpu.make_async_remote_copy(
                    src_ref=row_total.at[half], dst_ref=row_totals.at[at_x, half],
                    send_sem=row_send.at[d, half], recv_sem=row_recv.at[at_x, half],
                    device_id=device(at_x + d, at_y, 1), device_id_type=MESH,
                ))

    loads[3].wait()
    for j in range(8):
        weight[pl.ds(j, 16, stride=8), :] = residue_buf[:, pl.ds(128 * j, 128)]
    weight[...] = weight[...] * jnp.sqrt(one_minus_exp(2.0 * rate[...]))
    decays[0] = jnp.exp(-float(ROWS) * rate[...])
    decays[1] = jnp.exp(-float(2 * SIDE * ROWS) * rate[...])
    for core_at in range(2):
        decays[2 + core_at] = jnp.exp(rate[...] * (-float(ROWS) * (2 * at_y + core_at).astype(F32)))
    for block in range(ROWS // BLOCK):
        starts[block] = weight[...] * jnp.exp(rate[...] * -float(block * BLOCK))

    power = weight[...]
    for k in range(STEP):
        tap = power[0:8]
        for n in range(1, 16):
            tap = tap + power[8 * n : 8 * n + 8]
        taps[8 * k : 8 * k + 8, :] = tap
        power = power * ratio[...]

    def local(i, _):
        f = [row(taps, k) for k in range(STEP)]
        x = [row(xs, STEP * i + r) for r in range(STEP)]
        for r in range(STEP):
            y = f[r] * x[0]
            for k in range(1, r + 1):
                y = y + f[r - k] * x[k]
            ys[pl.ds(pl.multiple_of((STEP * i + r) * 8, 8), 8), :] = y
        rows = pl.ds(pl.multiple_of(i * 128, 128), 128)
        kept[rows, :] = kept[rows, :] * weight[...]
        return 0

    lax.fori_loop(0, ROWS // STEP, local, 0)

    @pl.when(is_second)
    def _():
        states[2 * at_y + 1, 0] = own[0]
        states[2 * at_y + 1, 1] = own[1]
        prefixes[0] = jnp.zeros((128, 128), F32)

        def wait_state(i, _):
            sender = lax.rem(2 * at_y + 2 + i, 2 * SIDE)
            for half in range(2):
                pltpu.make_async_remote_copy(
                    src_ref=own.at[half], dst_ref=states.at[sender, half], send_sem=state_send.at[half, 0],
                    recv_sem=state_recv.at[sender, half], device_id=other_core, device_id_type=MESH,
                ).wait_recv()
            return 0

        lax.fori_loop(0, 2 * SIDE - 1, wait_state, 0)
        for half in range(2):
            rows = pl.ds(64 * half, 64)
            device_decay = decays[0, rows, :]
            whole = states[0, half].astype(F32)
            for at in range(1, 2 * SIDE):
                prefixes[at, rows, :] = whole
                whole = device_decay * whole + states[at, half].astype(F32)
            row_total[half] = whole.astype(BF16)
            if half == 0:
                @pl.when(at_x < SIDE - 1)
                def _():
                    pl.semaphore_wait(row_ready, SIDE - 1 - at_x)

            row_copies(half, lambda copy: copy.start())

    def core_copy(half):
        return pltpu.make_async_remote_copy(
            src_ref=sent_before.at[half], dst_ref=before.at[half], send_sem=core_send.at[half], recv_sem=core_recv.at[half],
            device_id=other_core, device_id_type=MESH,
        )

    @pl.when(is_second)
    def _():
        for half in range(2):
            rows = pl.ds(64 * half, 64)
            row_decay = decays[1, rows, :]

            def add_row(x, state):
                pltpu.make_async_remote_copy(
                    src_ref=row_total.at[half], dst_ref=row_totals.at[x, half], send_sem=row_send.at[0, half],
                    recv_sem=row_recv.at[x, half], device_id=other_core, device_id_type=MESH,
                ).wait_recv()
                return row_decay * state + row_totals[x, half].astype(F32)

            rows_before = lax.fori_loop(0, at_x, add_row, jnp.zeros((64, 128), F32))
            sent_before[half] = decays[2, rows, :] * rows_before + prefixes[2 * at_y, rows, :]
            core_copy(half).start()
            before[half] = decays[3, rows, :] * rows_before + prefixes[2 * at_y + 1, rows, :]

    @pl.when(jnp.logical_not(is_second))
    def _():
        core_copy(0).wait_recv()
        core_copy(1).wait_recv()

    loads[4].wait()
    def gate(block):
        a = modes(ratio, 0) + modes(ratio, 1)

        def step(i, carried):
            at = block * (BLOCK // STEP) + i
            state = tuple(carried[n] + row(kept, at * 16 + n) for n in range(16))
            for r in range(STEP):
                t = STEP * at + r
                state = tuple(a[n] * state[n] for n in range(16))
                sums = [(state[4 * m] + state[4 * m + 1]) + (state[4 * m + 2] + state[4 * m + 3]) for m in range(4)]
                ys[pl.ds(pl.multiple_of(t * 8, 8), 8), :] = row(ys, t) + ((sums[0] + sums[1]) + (sums[2] + sums[3]))
            return tuple(carried[n] * row(ratio_step, n) for n in range(16))

        lax.fori_loop(0, BLOCK // STEP, step, tuple(
            before[n // 8, 8 * (n % 8) : 8 * (n % 8) + 8, :] * starts[block, 8 * n : 8 * n + 8, :] for n in range(16)
        ))

        def sixteen(i, _):
            rows = pl.ds(pl.multiple_of(block * BLOCK + i * 16, 16), 16)
            for j in range(8):
                lanes = pl.ds(128 * j, 128)
                y = ys[pl.ds((block * BLOCK + i * 16) * 8 + j, 16, stride=8), :]
                gated[rows, lanes] = (q_buf[rows, lanes].astype(F32) * y).astype(BF16)
            return 0

        lax.fori_loop(0, BLOCK // 16, sixteen, 0)

    def rows_of(block):
        return pl.ds(block * BLOCK, BLOCK)

    def z_copy(direction, at):
        return pltpu.make_async_remote_copy(
            src_ref=sent.at[direction, at], dst_ref=received.at[direction, at],
            send_sem=z_send.at[direction, at], recv_sem=z_recv.at[direction, at],
            device_id=z_neighbour(direction), device_id_type=MESH,
        )

    def turned_copy(block, at):
        return pltpu.make_async_remote_copy(
            src_ref=sent.at[0, at], dst_ref=turned.at[block], send_sem=turned_send.at[block], recv_sem=turned_recv.at[block],
            device_id=z_neighbour(1), device_id_type=MESH,
        )

    for rd in (4, 5, 3):
        w_loads[rd].wait()
    for at in range(4):
        block = ORDER[0][at][0]
        gate(block)
        for direction in range(2):
            product = jnp.dot(gated[rows_of(block), :], w_buf[relative(direction, block, 0)], preferred_element_type=F32)
            sent[direction, at] = product.astype(BF16)
            if block >= 1:
                z_copy(direction, at).start()
            elif direction == 0:
                @pl.when(is_from)
                def _():
                    turned_copy(block, at).start()

                @pl.when(jnp.logical_not(is_from))
                def _():
                    z_copy(direction, at).start()
            else:
                @pl.when(is_via)
                def _():
                    part[relative(direction, block, 0), rows_of(block), :] = product

                @pl.when(jnp.logical_not(is_via))
                def _():
                    z_copy(direction, at).start()

    def pass_on(block):
        at = INDEX[1][block, 0]

        @pl.when(is_via)
        def _():
            turned_copy(block, at).wait_recv()
            summed = part[relative(1, block, 0), rows_of(block), :] + turned[block].astype(F32)
            sent[1, at] = summed.astype(BF16)
            z_copy(1, at).start()

    def products(k, _):
        rd = jnp.where(lax.rem(k, 2) == 0, 3 - lax.div(k, 2), 5 + lax.div(k, 2))
        for n in range(2):
            lanes = pl.ds(256 * n, 256)
            part[rd, :, lanes] = jnp.dot(gated[...], w_buf[rd, :, lanes], preferred_element_type=F32)
        return 0

    for rd in (2, 6):
        w_loads[rd].wait()
    lax.fori_loop(0, 2, products, 0)
    pass_on(0)
    lax.fori_loop(2, 4, products, 0)

    for at in range(4, UNITS):
        if at == 8:
            for rd in (1, 7, 0):
                w_loads[rd].wait()
            lax.fori_loop(4, 7, products, 0)
        for direction in range(2):
            block, step = ORDER[direction][at]
            previous = INDEX[direction][block, step - 1]
            spared = direction == 0 and block < 1 and step == 1

            def add(direction=direction, at=at, block=block, step=step, previous=previous):
                z_copy(direction, previous).wait_recv()
                summed = part[relative(direction, block, step), rows_of(block), :] + received[direction, previous].astype(F32)
                sent[direction, at] = summed.astype(BF16)

            if spared:
                pl.when(jnp.logical_not(is_spared))(add)

                @pl.when(is_spared)
                def _():
                    sent[direction, at] = part[relative(direction, block, step), rows_of(block), :].astype(BF16)
            else:
                add()
            z_copy(direction, at).start()

    for block in (0, 2, 1, 3):
        summed = part[0, rows_of(block), :]
        for direction in range(2):
            last = INDEX[direction][block, HOPS[direction][block] - 1]
            z_copy(direction, last).wait_recv()
            summed = summed + received[direction, last].astype(F32)
        out[rows_of(block), :] = summed.astype(BF16)

    state_copies(0, lambda copy: copy.wait_send())
    state_copies(1, lambda copy: copy.wait_send())

    @pl.when(is_second)
    def _():
        for half in range(2):
            row_copies(half, lambda copy: copy.wait_send())
            core_copy(half).wait_send()

    for direction in range(2):
        for at in range(UNITS):
            block, step = ORDER[direction][at]
            if direction == 0 and block < 1 and step == 0:
                @pl.when(is_from)
                def _():
                    turned_copy(block, at).wait_send()

                @pl.when(jnp.logical_not(is_from))
                def _():
                    z_copy(direction, at).wait_send()
            else:
                z_copy(direction, at).wait_send()


def per_device(query_proj, key_projected, value_projected, mode_decay_speed, residue, out_weight):
    vmem, dma = pltpu.VMEM, pltpu.SemaphoreType.DMA
    operands = (query_proj, key_projected, value_projected, mode_decay_speed.T, residue.T, out_weight)
    return pl.pallas_call(
        kernel,
        out_shape=jax.ShapeDtypeStruct((ROWS, COLS), BF16),
        in_specs=[pl.BlockSpec(memory_space=pltpu.HBM)] * 6,
        out_specs=pl.BlockSpec(memory_space=pltpu.VMEM),
        scratch_shapes=[
            vmem((ROWS, WIDTH), BF16), vmem((ROWS, WIDTH), BF16), vmem((ROWS, WIDTH), BF16),
            vmem((16, WIDTH), F32), vmem((16, WIDTH), F32), vmem((8, WIDTH, COLS), BF16),
            vmem((128, 128), F32), vmem((128, 128), F32), vmem((128, 128), F32), vmem((128, 128), F32),
            vmem((4, 128, 128), F32), vmem((ROWS // BLOCK, 128, 128), F32), vmem((STEP * 8, 128), F32), vmem((ROWS // STEP * 128, 128), F32), vmem((ROWS * 8, 128), F32), vmem((ROWS * 8, 128), F32),
            vmem((2, 64, 128), BF16), vmem((2 * SIDE, 2, 64, 128), BF16), vmem((2, 64, 128), BF16), vmem((SIDE, 2, 64, 128), BF16),
            vmem((2 * SIDE, 128, 128), F32), vmem((2, 64, 128), F32), vmem((2, 64, 128), F32), vmem((ROWS, WIDTH), BF16), vmem((8, ROWS, COLS), F32),
            vmem((2, UNITS, BLOCK, COLS), BF16), vmem((2, UNITS, BLOCK, COLS), BF16), vmem((1, BLOCK, COLS), BF16),
            dma((5,)), dma((8,)), dma((2, SIDE)), dma((2 * SIDE, 2)), pltpu.SemaphoreType.REGULAR, dma((SIDE, 2)), dma((SIDE, 2)), dma((2,)), dma((2,)),
            dma((2, UNITS)), dma((2, UNITS)), dma((1,)), dma((1,)),
        ],
        compiler_params=pltpu.CompilerParams(collective_id=0, has_side_effects=True, vmem_limit_bytes=48 << 20),
        name="hyena",
    )(*(pltpu.with_memory_space_constraint(operand, pltpu.HBM) for operand in operands))


def solution(mesh):
    return jax.shard_map(
        per_device,
        mesh=mesh,
        in_specs=(P("seq", "ch"), P("seq", "ch"), P("seq", "ch"), P("ch", None), P("ch", None), P("ch", None)),
        out_specs=P("seq", "ch"),
        check_vma=False,
    )
```

```python
import jax
import jax.numpy as jnp
from jax import lax
from jax.experimental import pallas as pl
from jax.experimental.pallas import tpu as pltpu
from jax.sharding import PartitionSpec as P

MESH = pl.DeviceIdType.MESH
F32, BF16 = jnp.float32, jnp.bfloat16

ROWS = 256
WIDTH = 1024
COLS = 512
BLOCK = 64
STEP = 8
SIDE = 4

HOPS = ((4, 4, 3, 3), (3, 3, 4, 4))
ORDER = (
    ((0, 0), (2, 0), (1, 0), (3, 0), (0, 1), (1, 1), (2, 1), (3, 1), (0, 2), (1, 2), (2, 2), (3, 2), (0, 3), (1, 3)),
    ((0, 0), (2, 0), (1, 0), (3, 0), (2, 1), (1, 1), (3, 1), (0, 1), (2, 2), (3, 2), (1, 2), (0, 2), (2, 3), (3, 3)),
)
UNITS = len(ORDER[0])
TURNED = (5, 6, 7)
INDEX = tuple({unit: at for at, unit in enumerate(order)} for order in ORDER)


def relative(direction, block, step):
    left_over = HOPS[direction][block] - step
    return left_over if direction == 0 else 8 - left_over


def one_minus_exp(u):
    series = jnp.ones_like(u)
    for order in range(8, 1, -1):
        series = 1.0 - u * series * (1.0 / order)
    return jnp.where(u < 0.25, u * series, 1.0 - jnp.exp(-u))


def kernel(
    q_hbm, k_hbm, v_hbm, decay_hbm, residue_hbm, w_hbm, out,
    q_buf, k_buf, v_buf, decay_buf, residue_buf, w_buf,
    rate, ratio, ratio_step, weight, decays, starts, taps, kept, xs, ys, own, states, row_total, row_totals, prefixes, before, sent_before, gated, part, sent, received, turned,
    load_sem, w_sem, state_send, state_recv, row_ready, row_send, row_recv, core_send, core_recv, z_send, z_recv, turned_send, turned_recv,
):
    seq, z = lax.axis_index("seq"), lax.axis_index("ch")
    chip, core = lax.div(seq, 2), lax.rem(seq, 2)
    at_x, at_y = lax.div(chip, SIDE), lax.rem(chip, SIDE)
    is_second = core == 1

    def any_of(places):
        found = z == places[0]
        for place in places[1:]:
            found = found | (z == place)
        return found

    is_from = any_of(TURNED)
    is_via = any_of([place - 1 for place in TURNED])
    is_spared = any_of([(place + 1) % 8 for place in TURNED])

    def device(x, y, core_at):
        return {"seq": (x * SIDE + y) * 2 + core_at, "ch": z}

    def z_neighbour(direction):
        return {"seq": seq, "ch": lax.rem(z + (1 if direction == 0 else 7), 8)}

    other_core = device(at_x, at_y, 1 - core)

    loads = [
        pltpu.make_async_copy(source, target, load_sem.at[at])
        for at, (source, target) in enumerate(
            [(decay_hbm, decay_buf), (k_hbm, k_buf), (v_hbm, v_buf), (residue_hbm, residue_buf), (q_hbm, q_buf)]
        )
    ]
    for load in loads:
        load.start()

    barrier = pltpu.get_barrier_semaphore()
    def greet(partner):
        pl.semaphore_signal(barrier, inc=1, device_id=partner, device_id_type=MESH)

    greet(other_core)
    greet(z_neighbour(0))
    greet(z_neighbour(1))

    @pl.when(is_second)
    def _():
        for d in (2, 1, 3):
            near = lax.rem(at_y + d, SIDE)
            for partner in (device(at_x, near, 1), device(at_x, near, 0)):
                greet(partner)

        for d in range(1, SIDE):
            @pl.when(at_x + d < SIDE)
            def _():
                greet(device(at_x + d, at_y, 1))

    loads[0].wait()
    for j in range(8):
        rate[pl.ds(j, 16, stride=8), :] = decay_buf[:, pl.ds(128 * j, 128)]
    ratio[...] = jnp.exp(-rate[...])
    ratio_step[...] = jnp.exp(-float(STEP) * rate[...])

    loads[1].wait()
    loads[2].wait()
    w_loads = {}
    for rd in (4, 5, 3, 2, 6, 1, 7, 0):
        columns = pl.ds(pl.multiple_of(lax.rem(z + rd, 8) * COLS, COLS), COLS)
        w_loads[rd] = pltpu.make_async_copy(w_hbm.at[:, columns], w_buf.at[rd], w_sem.at[rd])
        w_loads[rd].start()

    def carrier_rows(i, _):
        rows = pl.ds(pl.multiple_of(i * 16, 16), 16)
        product = (k_buf[rows, :].astype(F32) * v_buf[rows, :].astype(F32)).astype(BF16).astype(F32)
        for j in range(8):
            xs[pl.ds(i * 128 + j, 16, stride=8), :] = product[:, 128 * j : 128 * j + 128]
        return 0

    lax.fori_loop(0, ROWS // 16, carrier_rows, 0)

    def row(ref, t):
        return ref[pl.ds(pl.multiple_of(t * 8, 8), 8), :]

    def modes(ref, half):
        return [row(ref, half * 8 + n) for n in range(8)]

    def own_state(half):
        a, a_step = modes(ratio, half), modes(ratio_step, half)

        def step(i, state):
            x = [row(xs, STEP * i + r) for r in range(STEP)]
            after = []
            for n in range(8):
                kept[pl.ds(pl.multiple_of((i * 16 + half * 8 + n) * 8, 8), 8), :] = state[n]
                added = x[0]
                for r in range(1, STEP):
                    added = added * a[n] + x[r]
                after.append(a_step[n] * state[n] + added)
            return tuple(after)

        state = lax.fori_loop(0, ROWS // STEP, step, tuple(jnp.zeros((8, 128), F32) for _ in range(8)))
        own[half] = jnp.concatenate(state, axis=0).astype(BF16)

    def state_copy(half, d):
        return pltpu.make_async_remote_copy(
            src_ref=own.at[half], dst_ref=states.at[2 * at_y + core, half],
            send_sem=state_send.at[half, d], recv_sem=state_recv.at[2 * at_y + core, half],
            device_id=device(at_x, lax.rem(at_y + d, SIDE), 1), device_id_type=MESH,
        )

    def state_copies(half, act):
        for d in (2, 3, 1):
            act(state_copy(half, d))

        @pl.when(jnp.logical_not(is_second))
        def _():
            act(state_copy(half, 0))

    own_state(0)
    @pl.when(is_second)
    def _():
        pl.semaphore_wait(barrier, SIDE - 1 + 3 + at_x)
        for d in range(1, SIDE):
            @pl.when(at_x >= d)
            def _():
                pl.semaphore_signal(row_ready, inc=1, device_id=device(at_x - d, at_y, 1), device_id_type=MESH)

    @pl.when(jnp.logical_not(is_second))
    def _():
        pl.semaphore_wait(barrier, SIDE + 2)

    state_copies(0, lambda copy: copy.start())
    own_state(1)
    state_copies(1, lambda copy: copy.start())

    def row_copies(half, act):
        for d in range(SIDE - 1, 0, -1):
            @pl.when(at_x + d < SIDE)
            def _():
                act(pltpu.make_async_remote_copy(
                    src_ref=row_total.at[half], dst_ref=row_totals.at[at_x, half],
                    send_sem=row_send.at[d, half], recv_sem=row_recv.at[at_x, half],
                    device_id=device(at_x + d, at_y, 1), device_id_type=MESH,
                ))

    loads[3].wait()
    for j in range(8):
        weight[pl.ds(j, 16, stride=8), :] = residue_buf[:, pl.ds(128 * j, 128)]
    weight[...] = weight[...] * jnp.sqrt(one_minus_exp(2.0 * rate[...]))
    decays[0] = jnp.exp(-float(ROWS) * rate[...])
    decays[1] = jnp.exp(-float(2 * SIDE * ROWS) * rate[...])
    for core_at in range(2):
        decays[2 + core_at] = jnp.exp(rate[...] * (-float(ROWS) * (2 * at_y + core_at).astype(F32)))
    for block in range(ROWS // BLOCK):
        starts[block] = weight[...] * jnp.exp(rate[...] * -float(block * BLOCK))

    power = weight[...]
    for k in range(STEP):
        tap = power[0:8]
        for n in range(1, 16):
            tap = tap + power[8 * n : 8 * n + 8]
        taps[8 * k : 8 * k + 8, :] = tap
        power = power * ratio[...]

    def local(i, _):
        f = [row(taps, k) for k in range(STEP)]
        x = [row(xs, STEP * i + r) for r in range(STEP)]
        for r in range(STEP):
            y = f[r] * x[0]
            for k in range(1, r + 1):
                y = y + f[r - k] * x[k]
            ys[pl.ds(pl.multiple_of((STEP * i + r) * 8, 8), 8), :] = y
        rows = pl.ds(pl.multiple_of(i * 128, 128), 128)
        kept[rows, :] = kept[rows, :] * weight[...]
        return 0

    lax.fori_loop(0, ROWS // STEP, local, 0)

    @pl.when(is_second)
    def _():
        states[2 * at_y + 1, 0] = own[0]
        states[2 * at_y + 1, 1] = own[1]
        prefixes[0] = jnp.zeros((128, 128), F32)

        def wait_state(i, _):
            sender = lax.rem(2 * at_y + 2 + i, 2 * SIDE)
            for half in range(2):
                pltpu.make_async_remote_copy(
                    src_ref=own.at[half], dst_ref=states.at[sender, half], send_sem=state_send.at[half, 0],
                    recv_sem=state_recv.at[sender, half], device_id=other_core, device_id_type=MESH,
                ).wait_recv()
            return 0

        lax.fori_loop(0, 2 * SIDE - 1, wait_state, 0)
        for half in range(2):
            rows = pl.ds(64 * half, 64)
            device_decay = decays[0, rows, :]
            whole = states[0, half].astype(F32)
            for at in range(1, 2 * SIDE):
                prefixes[at, rows, :] = whole
                whole = device_decay * whole + states[at, half].astype(F32)
            row_total[half] = whole.astype(BF16)
            if half == 0:
                @pl.when(at_x < SIDE - 1)
                def _():
                    pl.semaphore_wait(row_ready, SIDE - 1 - at_x)

            row_copies(half, lambda copy: copy.start())

    def core_copy(half):
        return pltpu.make_async_remote_copy(
            src_ref=sent_before.at[half], dst_ref=before.at[half], send_sem=core_send.at[half], recv_sem=core_recv.at[half],
            device_id=other_core, device_id_type=MESH,
        )

    @pl.when(is_second)
    def _():
        for half in range(2):
            rows = pl.ds(64 * half, 64)
            row_decay = decays[1, rows, :]

            def add_row(x, state):
                pltpu.make_async_remote_copy(
                    src_ref=row_total.at[half], dst_ref=row_totals.at[x, half], send_sem=row_send.at[0, half],
                    recv_sem=row_recv.at[x, half], device_id=other_core, device_id_type=MESH,
                ).wait_recv()
                return row_decay * state + row_totals[x, half].astype(F32)

            rows_before = lax.fori_loop(0, at_x, add_row, jnp.zeros((64, 128), F32))
            sent_before[half] = decays[2, rows, :] * rows_before + prefixes[2 * at_y, rows, :]
            core_copy(half).start()
            before[half] = decays[3, rows, :] * rows_before + prefixes[2 * at_y + 1, rows, :]

    @pl.when(jnp.logical_not(is_second))
    def _():
        core_copy(0).wait_recv()
        core_copy(1).wait_recv()

    loads[4].wait()
    def gate(block):
        a = modes(ratio, 0) + modes(ratio, 1)

        def step(i, carried):
            at = block * (BLOCK // STEP) + i
            state = tuple(carried[n] + row(kept, at * 16 + n) for n in range(16))
            for r in range(STEP):
                t = STEP * at + r
                state = tuple(a[n] * state[n] for n in range(16))
                sums = [(state[4 * m] + state[4 * m + 1]) + (state[4 * m + 2] + state[4 * m + 3]) for m in range(4)]
                ys[pl.ds(pl.multiple_of(t * 8, 8), 8), :] = row(ys, t) + ((sums[0] + sums[1]) + (sums[2] + sums[3]))
            return tuple(carried[n] * row(ratio_step, n) for n in range(16))

        lax.fori_loop(0, BLOCK // STEP, step, tuple(
            before[n // 8, 8 * (n % 8) : 8 * (n % 8) + 8, :] * starts[block, 8 * n : 8 * n + 8, :] for n in range(16)
        ))

        def sixteen(i, _):
            rows = pl.ds(pl.multiple_of(block * BLOCK + i * 16, 16), 16)
            for j in range(8):
                lanes = pl.ds(128 * j, 128)
                y = ys[pl.ds((block * BLOCK + i * 16) * 8 + j, 16, stride=8), :]
                gated[rows, lanes] = (q_buf[rows, lanes].astype(F32) * y).astype(BF16)
            return 0

        lax.fori_loop(0, BLOCK // 16, sixteen, 0)

    def rows_of(block):
        return pl.ds(block * BLOCK, BLOCK)

    def z_copy(direction, at):
        return pltpu.make_async_remote_copy(
            src_ref=sent.at[direction, at], dst_ref=received.at[direction, at],
            send_sem=z_send.at[direction, at], recv_sem=z_recv.at[direction, at],
            device_id=z_neighbour(direction), device_id_type=MESH,
        )

    def turned_copy(block, at):
        return pltpu.make_async_remote_copy(
            src_ref=sent.at[0, at], dst_ref=turned.at[block], send_sem=turned_send.at[block], recv_sem=turned_recv.at[block],
            device_id=z_neighbour(1), device_id_type=MESH,
        )

    for rd in (4, 5, 3):
        w_loads[rd].wait()
    def leave(direction, at):
        block = ORDER[0][at][0]
        product = jnp.dot(gated[rows_of(block), :], w_buf[relative(direction, block, 0)], preferred_element_type=F32)
        sent[direction, at] = product.astype(BF16)
        if block >= 1:
            z_copy(direction, at).start()
        elif direction == 0:
            @pl.when(is_from)
            def _():
                turned_copy(block, at).start()

            @pl.when(jnp.logical_not(is_from))
            def _():
                z_copy(direction, at).start()
        else:
            @pl.when(is_via)
            def _():
                part[relative(direction, block, 0), rows_of(block), :] = product

            @pl.when(jnp.logical_not(is_via))
            def _():
                z_copy(direction, at).start()

    gate(ORDER[0][0][0])
    leave(0, 0)
    gate(ORDER[0][1][0])
    leave(0, 1)
    leave(1, 0)
    gate(ORDER[0][2][0])
    leave(0, 2)
    leave(1, 1)
    gate(ORDER[0][3][0])
    leave(0, 3)
    leave(1, 2)
    leave(1, 3)

    def pass_on(block):
        at = INDEX[1][block, 0]

        @pl.when(is_via)
        def _():
            turned_copy(block, at).wait_recv()
            summed = part[relative(1, block, 0), rows_of(block), :] + turned[block].astype(F32)
            sent[1, at] = summed.astype(BF16)
            z_copy(1, at).start()

    def products(k, _):
        rd = jnp.where(lax.rem(k, 2) == 0, 3 - lax.div(k, 2), 5 + lax.div(k, 2))
        for n in range(2):
            lanes = pl.ds(256 * n, 256)
            part[rd, :, lanes] = jnp.dot(gated[...], w_buf[rd, :, lanes], preferred_element_type=F32)
        return 0

    for rd in (2, 6):
        w_loads[rd].wait()
    lax.fori_loop(0, 2, products, 0)
    pass_on(0)
    lax.fori_loop(2, 4, products, 0)

    for at in range(4, UNITS):
        if at == 8:
            for rd in (1, 7, 0):
                w_loads[rd].wait()
            lax.fori_loop(4, 7, products, 0)
        for direction in range(2):
            block, step = ORDER[direction][at]
            previous = INDEX[direction][block, step - 1]
            spared = direction == 0 and block < 1 and step == 1

            def add(direction=direction, at=at, block=block, step=step, previous=previous):
                z_copy(direction, previous).wait_recv()
                summed = part[relative(direction, block, step), rows_of(block), :] + received[direction, previous].astype(F32)
                sent[direction, at] = summed.astype(BF16)

            if spared:
                pl.when(jnp.logical_not(is_spared))(add)

                @pl.when(is_spared)
                def _():
                    sent[direction, at] = part[relative(direction, block, step), rows_of(block), :].astype(BF16)
            else:
                add()
            z_copy(direction, at).start()

    for block in (0, 2, 1, 3):
        summed = part[0, rows_of(block), :]
        for direction in range(2):
            last = INDEX[direction][block, HOPS[direction][block] - 1]
            z_copy(direction, last).wait_recv()
            summed = summed + received[direction, last].astype(F32)
        out[rows_of(block), :] = summed.astype(BF16)

    state_copies(0, lambda copy: copy.wait_send())
    state_copies(1, lambda copy: copy.wait_send())

    @pl.when(is_second)
    def _():
        for half in range(2):
            row_copies(half, lambda copy: copy.wait_send())
            core_copy(half).wait_send()

    for direction in range(2):
        for at in range(UNITS):
            block, step = ORDER[direction][at]
            if direction == 0 and block < 1 and step == 0:
                @pl.when(is_from)
                def _():
                    turned_copy(block, at).wait_send()

                @pl.when(jnp.logical_not(is_from))
                def _():
                    z_copy(direction, at).wait_send()
            else:
                z_copy(direction, at).wait_send()


def per_device(query_proj, key_projected, value_projected, mode_decay_speed, residue, out_weight):
    vmem, dma = pltpu.VMEM, pltpu.SemaphoreType.DMA
    operands = (query_proj, key_projected, value_projected, mode_decay_speed.T, residue.T, out_weight)
    return pl.pallas_call(
        kernel,
        out_shape=jax.ShapeDtypeStruct((ROWS, COLS), BF16),
        in_specs=[pl.BlockSpec(memory_space=pltpu.HBM)] * 6,
        out_specs=pl.BlockSpec(memory_space=pltpu.VMEM),
        scratch_shapes=[
            vmem((ROWS, WIDTH), BF16), vmem((ROWS, WIDTH), BF16), vmem((ROWS, WIDTH), BF16),
            vmem((16, WIDTH), F32), vmem((16, WIDTH), F32), vmem((8, WIDTH, COLS), BF16),
            vmem((128, 128), F32), vmem((128, 128), F32), vmem((128, 128), F32), vmem((128, 128), F32),
            vmem((4, 128, 128), F32), vmem((ROWS // BLOCK, 128, 128), F32), vmem((STEP * 8, 128), F32), vmem((ROWS // STEP * 128, 128), F32), vmem((ROWS * 8, 128), F32), vmem((ROWS * 8, 128), F32),
            vmem((2, 64, 128), BF16), vmem((2 * SIDE, 2, 64, 128), BF16), vmem((2, 64, 128), BF16), vmem((SIDE, 2, 64, 128), BF16),
            vmem((2 * SIDE, 128, 128), F32), vmem((2, 64, 128), F32), vmem((2, 64, 128), F32), vmem((ROWS, WIDTH), BF16), vmem((8, ROWS, COLS), F32),
            vmem((2, UNITS, BLOCK, COLS), BF16), vmem((2, UNITS, BLOCK, COLS), BF16), vmem((1, BLOCK, COLS), BF16),
            dma((5,)), dma((8,)), dma((2, SIDE)), dma((2 * SIDE, 2)), pltpu.SemaphoreType.REGULAR, dma((SIDE, 2)), dma((SIDE, 2)), dma((2,)), dma((2,)),
            dma((2, UNITS)), dma((2, UNITS)), dma((1,)), dma((1,)),
        ],
        compiler_params=pltpu.CompilerParams(collective_id=0, has_side_effects=True, vmem_limit_bytes=48 << 20),
        name="hyena",
    )(*(pltpu.with_memory_space_constraint(operand, pltpu.HBM) for operand in operands))


def solution(mesh):
    return jax.shard_map(
        per_device,
        mesh=mesh,
        in_specs=(P("seq", "ch"), P("seq", "ch"), P("seq", "ch"), P("ch", None), P("ch", None), P("ch", None)),
        out_specs=P("seq", "ch"),
        check_vma=False,
    )
```

```python
import jax
import jax.numpy as jnp
from jax import lax
from jax.experimental import pallas as pl
from jax.experimental.pallas import tpu as pltpu
from jax.sharding import PartitionSpec as P

MESH = pl.DeviceIdType.MESH
F32, BF16 = jnp.float32, jnp.bfloat16

ROWS = 256
WIDTH = 1024
COLS = 512
BLOCK = 64
STEP = 8
SIDE = 4

HOPS = ((4, 4, 3, 3), (3, 3, 4, 4))
ORDER = (
    ((0, 0), (2, 0), (1, 0), (3, 0), (0, 1), (1, 1), (2, 1), (3, 1), (0, 2), (1, 2), (2, 2), (3, 2), (0, 3), (1, 3)),
    ((0, 0), (2, 0), (1, 0), (3, 0), (2, 1), (1, 1), (3, 1), (0, 1), (2, 2), (3, 2), (1, 2), (0, 2), (2, 3), (3, 3)),
)
UNITS = len(ORDER[0])
TURNED = (5, 6, 7)
INDEX = tuple({unit: at for at, unit in enumerate(order)} for order in ORDER)


def relative(direction, block, step):
    left_over = HOPS[direction][block] - step
    return left_over if direction == 0 else 8 - left_over


def one_minus_exp(u):
    series = jnp.ones_like(u)
    for order in range(8, 1, -1):
        series = 1.0 - u * series * (1.0 / order)
    return jnp.where(u < 0.25, u * series, 1.0 - jnp.exp(-u))


def kernel(
    q_hbm, k_hbm, v_hbm, decay_hbm, residue_hbm, w_hbm, out,
    q_buf, k_buf, v_buf, decay_buf, residue_buf, w_buf,
    staged, rate, ratio, ratio_step, weight, decays, starts, taps, kept, xs, ys, own, states, row_total, row_totals, prefixes, before, sent_before, gated, part, sent, received, turned,
    load_sem, w_sem, state_send, state_recv, row_ready, row_send, row_recv, core_send, core_recv, z_send, z_recv, turned_send, turned_recv,
):
    seq, z = lax.axis_index("seq"), lax.axis_index("ch")
    chip, core = lax.div(seq, 2), lax.rem(seq, 2)
    at_x, at_y = lax.div(chip, SIDE), lax.rem(chip, SIDE)
    is_second = core == 1

    def any_of(places):
        found = z == places[0]
        for place in places[1:]:
            found = found | (z == place)
        return found

    is_from = any_of(TURNED)
    is_via = any_of([place - 1 for place in TURNED])
    is_spared = any_of([(place + 1) % 8 for place in TURNED])

    def device(x, y, core_at):
        return {"seq": (x * SIDE + y) * 2 + core_at, "ch": z}

    def z_neighbour(direction):
        return {"seq": seq, "ch": lax.rem(z + (1 if direction == 0 else 7), 8)}

    other_core = device(at_x, at_y, 1 - core)

    loads = [
        pltpu.make_async_copy(source, target, load_sem.at[at])
        for at, (source, target) in enumerate(
            [(decay_hbm, decay_buf), (k_hbm, k_buf), (v_hbm, v_buf), (residue_hbm, residue_buf), (q_hbm, q_buf)]
        )
    ]
    for load in loads:
        load.start()

    barrier = pltpu.get_barrier_semaphore()
    def greet(partner):
        pl.semaphore_signal(barrier, inc=1, device_id=partner, device_id_type=MESH)

    greet(other_core)
    greet(z_neighbour(0))
    greet(z_neighbour(1))

    @pl.when(is_second)
    def _():
        for d in (2, 1, 3):
            near = lax.rem(at_y + d, SIDE)
            for partner in (device(at_x, near, 1), device(at_x, near, 0)):
                greet(partner)

        for d in range(1, SIDE):
            @pl.when(at_x + d < SIDE)
            def _():
                greet(device(at_x + d, at_y, 1))

    loads[0].wait()
    for j in range(8):
        staged[pl.ds(j, 16, stride=8), :] = decay_buf[:, pl.ds(128 * j, 128)]
    rate[...] = staged[pl.ds(0, 128), :]
    ratio[...] = jnp.exp(-rate[...])
    ratio_step[...] = jnp.exp(-float(STEP) * rate[...])

    loads[1].wait()
    loads[2].wait()
    w_loads = {}
    for rd in (4, 5, 3, 2, 6, 1, 7, 0):
        columns = pl.ds(pl.multiple_of(lax.rem(z + rd, 8) * COLS, COLS), COLS)
        w_loads[rd] = pltpu.make_async_copy(w_hbm.at[:, columns], w_buf.at[rd], w_sem.at[rd])
        w_loads[rd].start()

    def carrier_rows(i, _):
        rows = pl.ds(pl.multiple_of(i * 16, 16), 16)
        product = (k_buf[rows, :].astype(F32) * v_buf[rows, :].astype(F32)).astype(BF16).astype(F32)
        for j in range(8):
            xs[pl.ds(i * 128 + j, 16, stride=8), :] = product[:, 128 * j : 128 * j + 128]
        return 0

    lax.fori_loop(0, ROWS // 16, carrier_rows, 0)

    def row(ref, t):
        return ref[pl.ds(pl.multiple_of(t * 8, 8), 8), :]

    def modes(ref, half):
        return [row(ref, half * 8 + n) for n in range(8)]

    def own_state(half):
        a, a_step = modes(ratio, half), modes(ratio_step, half)

        def step(i, state):
            x = [row(xs, STEP * i + r) for r in range(STEP)]
            after = []
            for n in range(8):
                kept[pl.ds(pl.multiple_of((i * 16 + half * 8 + n) * 8, 8), 8), :] = state[n]
                added = x[0]
                for r in range(1, STEP):
                    added = added * a[n] + x[r]
                after.append(a_step[n] * state[n] + added)
            return tuple(after)

        state = lax.fori_loop(0, ROWS // STEP, step, tuple(jnp.zeros((8, 128), F32) for _ in range(8)))
        own[half] = jnp.concatenate(state, axis=0).astype(BF16)

    def state_copy(half, d):
        return pltpu.make_async_remote_copy(
            src_ref=own.at[half], dst_ref=states.at[2 * at_y + core, half],
            send_sem=state_send.at[half, d], recv_sem=state_recv.at[2 * at_y + core, half],
            device_id=device(at_x, lax.rem(at_y + d, SIDE), 1), device_id_type=MESH,
        )

    def state_copies(half, act):
        for d in (2, 3, 1):
            act(state_copy(half, d))

        @pl.when(jnp.logical_not(is_second))
        def _():
            act(state_copy(half, 0))

    own_state(0)
    @pl.when(is_second)
    def _():
        pl.semaphore_wait(barrier, SIDE - 1 + 3 + at_x)
        for d in range(1, SIDE):
            @pl.when(at_x >= d)
            def _():
                pl.semaphore_signal(row_ready, inc=1, device_id=device(at_x - d, at_y, 1), device_id_type=MESH)

    @pl.when(jnp.logical_not(is_second))
    def _():
        pl.semaphore_wait(barrier, SIDE + 2)

    state_copies(0, lambda copy: copy.start())
    own_state(1)
    state_copies(1, lambda copy: copy.start())

    def row_copies(half, act):
        for d in range(SIDE - 1, 0, -1):
            @pl.when(at_x + d < SIDE)
            def _():
                act(pltpu.make_async_remote_copy(
                    src_ref=row_total.at[half], dst_ref=row_totals.at[at_x, half],
                    send_sem=row_send.at[d, half], recv_sem=row_recv.at[at_x, half],
                    device_id=device(at_x + d, at_y, 1), device_id_type=MESH,
                ))

    loads[3].wait()
    for j in range(8):
        staged[pl.ds(j, 16, stride=8), :] = residue_buf[:, pl.ds(128 * j, 128)]
    weight[...] = staged[pl.ds(0, 128), :] * jnp.sqrt(one_minus_exp(2.0 * rate[...]))
    decays[0] = jnp.exp(-float(ROWS) * rate[...])
    decays[1] = jnp.exp(-float(2 * SIDE * ROWS) * rate[...])
    for core_at in range(2):
        decays[2 + core_at] = jnp.exp(rate[...] * (-float(ROWS) * (2 * at_y + core_at).astype(F32)))
    for block in range(ROWS // BLOCK):
        starts[block] = weight[...] * jnp.exp(rate[...] * -float(block * BLOCK))

    power = weight[...]
    for k in range(STEP):
        tap = power[0:8]
        for n in range(1, 16):
            tap = tap + power[8 * n : 8 * n + 8]
        taps[8 * k : 8 * k + 8, :] = tap
        power = power * ratio[...]

    def local(i, _):
        f = [row(taps, k) for k in range(STEP)]
        x = [row(xs, STEP * i + r) for r in range(STEP)]
        for r in range(STEP):
            y = f[r] * x[0]
            for k in range(1, r + 1):
                y = y + f[r - k] * x[k]
            ys[pl.ds(pl.multiple_of((STEP * i + r) * 8, 8), 8), :] = y
        rows = pl.ds(pl.multiple_of(i * 128, 128), 128)
        kept[rows, :] = kept[rows, :] * weight[...]
        return 0

    lax.fori_loop(0, ROWS // STEP, local, 0)

    @pl.when(is_second)
    def _():
        states[2 * at_y + 1, 0] = own[0]
        states[2 * at_y + 1, 1] = own[1]
        prefixes[0] = jnp.zeros((128, 128), F32)

        def wait_state(i, _):
            sender = lax.rem(2 * at_y + 2 + i, 2 * SIDE)
            for half in range(2):
                pltpu.make_async_remote_copy(
                    src_ref=own.at[half], dst_ref=states.at[sender, half], send_sem=state_send.at[half, 0],
                    recv_sem=state_recv.at[sender, half], device_id=other_core, device_id_type=MESH,
                ).wait_recv()
            return 0

        lax.fori_loop(0, 2 * SIDE - 1, wait_state, 0)
        for half in range(2):
            rows = pl.ds(64 * half, 64)
            device_decay = decays[0, rows, :]
            whole = states[0, half].astype(F32)
            for at in range(1, 2 * SIDE):
                prefixes[at, rows, :] = whole
                whole = device_decay * whole + states[at, half].astype(F32)
            row_total[half] = whole.astype(BF16)
            if half == 0:
                @pl.when(at_x < SIDE - 1)
                def _():
                    pl.semaphore_wait(row_ready, SIDE - 1 - at_x)

            row_copies(half, lambda copy: copy.start())

    def core_copy(half):
        return pltpu.make_async_remote_copy(
            src_ref=sent_before.at[half], dst_ref=before.at[half], send_sem=core_send.at[half], recv_sem=core_recv.at[half],
            device_id=other_core, device_id_type=MESH,
        )

    @pl.when(is_second)
    def _():
        for half in range(2):
            rows = pl.ds(64 * half, 64)
            row_decay = decays[1, rows, :]

            def add_row(x, state):
                pltpu.make_async_remote_copy(
                    src_ref=row_total.at[half], dst_ref=row_totals.at[x, half], send_sem=row_send.at[0, half],
                    recv_sem=row_recv.at[x, half], device_id=other_core, device_id_type=MESH,
                ).wait_recv()
                return row_decay * state + row_totals[x, half].astype(F32)

            rows_before = lax.fori_loop(0, at_x, add_row, jnp.zeros((64, 128), F32))
            sent_before[half] = decays[2, rows, :] * rows_before + prefixes[2 * at_y, rows, :]
            core_copy(half).start()
            before[half] = decays[3, rows, :] * rows_before + prefixes[2 * at_y + 1, rows, :]

    @pl.when(jnp.logical_not(is_second))
    def _():
        core_copy(0).wait_recv()
        core_copy(1).wait_recv()

    loads[4].wait()
    def gate(block):
        a = modes(ratio, 0) + modes(ratio, 1)

        def step(i, carried):
            at = block * (BLOCK // STEP) + i
            state = tuple(carried[n] + row(kept, at * 16 + n) for n in range(16))
            for r in range(STEP):
                t = STEP * at + r
                state = tuple(a[n] * state[n] for n in range(16))
                sums = [(state[4 * m] + state[4 * m + 1]) + (state[4 * m + 2] + state[4 * m + 3]) for m in range(4)]
                ys[pl.ds(pl.multiple_of(t * 8, 8), 8), :] = row(ys, t) + ((sums[0] + sums[1]) + (sums[2] + sums[3]))
            return tuple(carried[n] * row(ratio_step, n) for n in range(16))

        lax.fori_loop(0, BLOCK // STEP, step, tuple(
            before[n // 8, 8 * (n % 8) : 8 * (n % 8) + 8, :] * starts[block, 8 * n : 8 * n + 8, :] for n in range(16)
        ))

        def sixteen(i, _):
            rows = pl.ds(pl.multiple_of(block * BLOCK + i * 16, 16), 16)
            for j in range(8):
                lanes = pl.ds(128 * j, 128)
                y = ys[pl.ds((block * BLOCK + i * 16) * 8 + j, 16, stride=8), :]
                gated[rows, lanes] = (q_buf[rows, lanes].astype(F32) * y).astype(BF16)
            return 0

        lax.fori_loop(0, BLOCK // 16, sixteen, 0)

    def rows_of(block):
        return pl.ds(block * BLOCK, BLOCK)

    def z_copy(direction, at):
        return pltpu.make_async_remote_copy(
            src_ref=sent.at[direction, at], dst_ref=received.at[direction, at],
            send_sem=z_send.at[direction, at], recv_sem=z_recv.at[direction, at],
            device_id=z_neighbour(direction), device_id_type=MESH,
        )

    def turned_copy(block, at):
        return pltpu.make_async_remote_copy(
            src_ref=sent.at[0, at], dst_ref=turned.at[block], send_sem=turned_send.at[block], recv_sem=turned_recv.at[block],
            device_id=z_neighbour(1), device_id_type=MESH,
        )

    for rd in (4, 5, 3):
        w_loads[rd].wait()
    def leave(direction, at):
        block = ORDER[0][at][0]
        product = jnp.dot(gated[rows_of(block), :], w_buf[relative(direction, block, 0)], preferred_element_type=F32)
        sent[direction, at] = product.astype(BF16)
        if block >= 1:
            z_copy(direction, at).start()
        elif direction == 0:
            @pl.when(is_from)
            def _():
                turned_copy(block, at).start()

            @pl.when(jnp.logical_not(is_from))
            def _():
                z_copy(direction, at).start()
        else:
            @pl.when(is_via)
            def _():
                part[relative(direction, block, 0), rows_of(block), :] = product

            @pl.when(jnp.logical_not(is_via))
            def _():
                z_copy(direction, at).start()

    gate(ORDER[0][0][0])
    leave(0, 0)
    gate(ORDER[0][1][0])
    leave(0, 1)
    leave(1, 0)
    gate(ORDER[0][2][0])
    leave(0, 2)
    leave(1, 1)
    gate(ORDER[0][3][0])
    leave(0, 3)
    leave(1, 2)
    leave(1, 3)

    def pass_on(block):
        at = INDEX[1][block, 0]

        @pl.when(is_via)
        def _():
            turned_copy(block, at).wait_recv()
            summed = part[relative(1, block, 0), rows_of(block), :] + turned[block].astype(F32)
            sent[1, at] = summed.astype(BF16)
            z_copy(1, at).start()

    def products(k, _):
        rd = jnp.where(lax.rem(k, 2) == 0, 3 - lax.div(k, 2), 5 + lax.div(k, 2))
        for n in range(2):
            lanes = pl.ds(256 * n, 256)
            part[rd, :, lanes] = jnp.dot(gated[...], w_buf[rd, :, lanes], preferred_element_type=F32)
        return 0

    for rd in (2, 6):
        w_loads[rd].wait()
    lax.fori_loop(0, 2, products, 0)
    pass_on(0)
    lax.fori_loop(2, 4, products, 0)

    for at in range(4, UNITS):
        if at == 8:
            for rd in (1, 7, 0):
                w_loads[rd].wait()
            lax.fori_loop(4, 7, products, 0)
        for direction in range(2):
            block, step = ORDER[direction][at]
            previous = INDEX[direction][block, step - 1]
            spared = direction == 0 and block < 1 and step == 1

            def add(direction=direction, at=at, block=block, step=step, previous=previous):
                z_copy(direction, previous).wait_recv()
                summed = part[relative(direction, block, step), rows_of(block), :] + received[direction, previous].astype(F32)
                sent[direction, at] = summed.astype(BF16)

            if spared:
                pl.when(jnp.logical_not(is_spared))(add)

                @pl.when(is_spared)
                def _():
                    sent[direction, at] = part[relative(direction, block, step), rows_of(block), :].astype(BF16)
            else:
                add()
            z_copy(direction, at).start()

    for block in (0, 2, 1, 3):
        summed = part[0, rows_of(block), :]
        for direction in range(2):
            last = INDEX[direction][block, HOPS[direction][block] - 1]
            z_copy(direction, last).wait_recv()
            summed = summed + received[direction, last].astype(F32)
        out[rows_of(block), :] = summed.astype(BF16)

    state_copies(0, lambda copy: copy.wait_send())
    state_copies(1, lambda copy: copy.wait_send())

    @pl.when(is_second)
    def _():
        for half in range(2):
            row_copies(half, lambda copy: copy.wait_send())
            core_copy(half).wait_send()

    for direction in range(2):
        for at in range(UNITS):
            block, step = ORDER[direction][at]
            if direction == 0 and block < 1 and step == 0:
                @pl.when(is_from)
                def _():
                    turned_copy(block, at).wait_send()

                @pl.when(jnp.logical_not(is_from))
                def _():
                    z_copy(direction, at).wait_send()
            else:
                z_copy(direction, at).wait_send()


def per_device(query_proj, key_projected, value_projected, mode_decay_speed, residue, out_weight):
    vmem, dma = pltpu.VMEM, pltpu.SemaphoreType.DMA
    operands = (query_proj, key_projected, value_projected, mode_decay_speed.T, residue.T, out_weight)
    return pl.pallas_call(
        kernel,
        out_shape=jax.ShapeDtypeStruct((ROWS, COLS), BF16),
        in_specs=[pl.BlockSpec(memory_space=pltpu.HBM)] * 6,
        out_specs=pl.BlockSpec(memory_space=pltpu.VMEM),
        scratch_shapes=[
            vmem((ROWS, WIDTH), BF16), vmem((ROWS, WIDTH), BF16), vmem((ROWS, WIDTH), BF16),
            vmem((16, WIDTH), F32), vmem((16, WIDTH), F32), vmem((8, WIDTH, COLS), BF16),
            vmem((136, 128), F32),
            vmem((128, 128), F32), vmem((128, 128), F32), vmem((128, 128), F32), vmem((128, 128), F32),
            vmem((4, 128, 128), F32), vmem((ROWS // BLOCK, 128, 128), F32), vmem((STEP * 8, 128), F32), vmem((ROWS // STEP * 128, 128), F32), vmem((ROWS * 8 + 8, 128), F32), vmem((ROWS * 8 + 8, 128), F32),
            vmem((2, 64, 128), BF16), vmem((2 * SIDE, 2, 64, 128), BF16), vmem((2, 64, 128), BF16), vmem((SIDE, 2, 64, 128), BF16),
            vmem((2 * SIDE, 128, 128), F32), vmem((2, 64, 128), F32), vmem((2, 64, 128), F32), vmem((ROWS, WIDTH), BF16), vmem((8, ROWS, COLS), F32),
            vmem((2, UNITS, BLOCK, COLS), BF16), vmem((2, UNITS, BLOCK, COLS), BF16), vmem((1, BLOCK, COLS), BF16),
            dma((5,)), dma((8,)), dma((2, SIDE)), dma((2 * SIDE, 2)), pltpu.SemaphoreType.REGULAR, dma((SIDE, 2)), dma((SIDE, 2)), dma((2,)), dma((2,)),
            dma((2, UNITS)), dma((2, UNITS)), dma((1,)), dma((1,)),
        ],
        compiler_params=pltpu.CompilerParams(collective_id=0, has_side_effects=True, vmem_limit_bytes=48 << 20),
        name="hyena",
    )(*(pltpu.with_memory_space_constraint(operand, pltpu.HBM) for operand in operands))


def solution(mesh):
    return jax.shard_map(
        per_device,
        mesh=mesh,
        in_specs=(P("seq", "ch"), P("seq", "ch"), P("seq", "ch"), P("ch", None), P("ch", None), P("ch", None)),
        out_specs=P("seq", "ch"),
        check_vma=False,
    )
```
